32 devices in a mesh: clu: 4 (over y, x), mem: 8 (over z, core).
Axes of the slice: x: 2, y: 2, z: 4, core: 2. Of those that a mesh axis runs over, the one named last changes fastest.
Arguments:
- embeddings: bfloat16 [32768, 768], P(('clu', 'mem'))
- block_order: int32 [4, 64], P('clu'), may hold values from 0 to 7, as said below
Outputs:
- weight: float32 [32768], P(('clu', 'mem'))
The draws below stay inside these ranges and needn't reach their ends.
Inputs may be any that keep to these rules, and one draw needn't show every extreme that they name: `block_order`: each aligned run of 8 entries is a permutation of 0 to 7.
All inputs are finite; a program needn't handle non-finite values.
Results may differ from the reference program's by a relative error of at most 0.0029.
Values may be sent and summed in bfloat16 or wider, within the bound.
A program may use at most 64 MiB of HBM per device.

```python
import math
import jax
import jax.numpy as jnp
from jax import lax

D = 768
BLK = 128
BPD = 8
GBLK = 64
GROUPS = 4
ROWS = 32768
N_CLU = 4
N_MEM = 8


def draw_embeddings(key, part):
    centers_count = max(GBLK * BLK // 32, 2)
    supers_count = 8
    group_rows = GBLK * BLK
    key_label = jax.random.fold_in(key, 31)
    key_jitter = jax.random.fold_in(key, 32)
    key_noise = jax.random.fold_in(key, 33)
    key_subsq = jax.random.fold_in(key, 34)
    key_center = jax.random.fold_in(key, 35)
    key_parent = jax.random.fold_in(key, 36)
    key_supsq = jax.random.fold_in(key, 37)
    key_super = jax.random.fold_in(key, 38)
    key_common = jax.random.fold_in(key, 39)
    key_axes = jax.random.fold_in(key, 40)
    labels = jax.random.randint(key_label, (ROWS,), 0, centers_count)
    parents = jax.random.randint(key_parent, (centers_count,), 0, supers_count)
    position = jnp.arange(ROWS, dtype=jnp.float32) / ROWS
    jitter = jax.random.uniform(key_jitter, (ROWS,), jnp.float32)
    spread = 0.6 * position + 0.4 * jitter
    sigma_sq = 0.3 * jnp.power(8.0, spread)
    noise = jax.random.normal(key_noise, (ROWS, D), jnp.float32)
    center_noise = jax.random.normal(key_center, (centers_count, D), jnp.float32)
    super_noise = jax.random.normal(key_super, (supers_count, D), jnp.float32)
    common_noise = jax.random.normal(key_common, (GROUPS, D), jnp.float32)
    scale_low = 0.4
    scale_high = 1.6
    sub_low = 2.0
    sub_high = 8.0
    super_low = 1.0
    super_high = 6.0
    common_sq = 6.0
    scale_mean = (scale_high * scale_high - scale_low * scale_low) / (2.0 * math.log(scale_high / scale_low))
    axis_log = jax.random.uniform(key_axes, (D,), jnp.float32, math.log(scale_low), math.log(scale_high))
    axis_scale = jnp.exp(axis_log) / math.sqrt(scale_mean)
    root_width = jnp.sqrt(jnp.float32(D))
    sub_sq = jnp.exp(jax.random.uniform(key_subsq, (centers_count,), jnp.float32, math.log(sub_low), math.log(sub_high)))
    super_sq = jnp.exp(jax.random.uniform(key_supsq, (supers_count,), jnp.float32, math.log(super_low), math.log(super_high)))
    centers = center_noise * jnp.sqrt(sub_sq)[:, None] * axis_scale[None, :] / root_width
    supers = super_noise * jnp.sqrt(super_sq)[:, None] * axis_scale[None, :] / root_width
    commons = common_noise * math.sqrt(common_sq) * axis_scale[None, :] / root_width
    values = centers[labels] + supers[parents[labels]] + jnp.sqrt(sigma_sq)[:, None] * noise / root_width
    values = values.reshape(GROUPS, group_rows, D) + commons[:, None, :]
    return values.reshape(ROWS, D).astype(jnp.bfloat16)


def draw_block_order(key, part):
    runs = GROUPS * GBLK // BPD
    run_keys = jax.random.split(jax.random.fold_in(key, 21), runs)
    orders = jax.vmap(lambda one_key: jax.random.permutation(one_key, BPD))(run_keys)
    return orders.reshape(GROUPS, GBLK).astype(jnp.int32)


def setup_inputs(seed: int = 0) -> dict:
    splits = jax.random.split(jax.random.key(seed), 3)
    return {
        "embeddings": draw_embeddings(jax.random.fold_in(splits[2], 71), 0),
        "block_order": draw_block_order(jax.random.fold_in(splits[2], 71), 0),
    }


def class_table(count):
    spots = jnp.arange(count, dtype=jnp.int32)
    levels = count.bit_length() - 1
    classes = jnp.zeros((count,), jnp.int32)
    for level in range(1, levels + 1):
        classes = classes + (spots >= count - (count >> level)).astype(jnp.int32)
    return classes


def group_density(group_rows, group_ids):
    row_ids = jnp.repeat(group_ids, BLK)
    norms = jnp.sum(jnp.square(group_rows.astype(jnp.float32)), axis=1)
    block_len = BPD * BLK
    block_count = group_rows.shape[0] // block_len

    def one_block(index):
        start = (index * block_len).astype(jnp.int32)
        block = lax.dynamic_slice_in_dim(group_rows, start, block_len, 0)
        block_ids = lax.dynamic_slice_in_dim(row_ids, start, block_len, 0)
        block_norms = lax.dynamic_slice_in_dim(norms, start, block_len, 0)
        products = jnp.dot(block, group_rows.T, preferred_element_type=jnp.float32)
        distance = block_norms[:, None] + norms[None, :] - 2.0 * products
        kernel = jnp.where(block_ids[:, None] == row_ids[None, :], jnp.exp(-0.5 * distance), jnp.float32(0.0))
        return jnp.sum(kernel, axis=1)

    return lax.map(one_block, jnp.arange(block_count, dtype=jnp.int32)).reshape(-1)


def reference(embeddings, block_order):
    orders = block_order.reshape(N_CLU, N_MEM, BPD)
    classes = class_table(BPD)
    locals_range = jnp.arange(BPD, dtype=jnp.int32)
    matches = (orders[:, :, :, None] == locals_range[None, None, None, :]).astype(jnp.int32)
    local_class = jnp.sum(matches * classes[None, None, :, None], axis=2)
    group_ids = local_class.reshape(N_CLU, GBLK)
    grouped = embeddings.reshape(N_CLU, -1, D)
    density = lax.map(lambda pair: group_density(pair[0], pair[1]), (grouped, group_ids))
    inverse = 1.0 / density
    weight = inverse * (jnp.float32(ROWS) / jnp.sum(inverse))
    return weight.reshape(-1)
```

```python
import functools

import jax
import jax.numpy as jnp
from jax import lax
from jax.experimental import pallas as pl
from jax.experimental.pallas import tpu as pltpu
from jax.sharding import PartitionSpec as P

BLK = 128
PER = 8
HALF = PER // 2
UNIT = 2 * BLK
MESH = pl.DeviceIdType.MESH


def kernel(
    groups, members, order_ref, emb_ref, out_ref,
    mine, buf, rowacc, colacc, hcol, result, sums, weights,
    send_sem, recv_sem, sum_send, sum_recv, back_send, back_recv,
):
    chips = members // 2
    mid = chips // 2
    clu = lax.axis_index("clu")
    mem = lax.axis_index("mem")
    chip, core = mem // 2, mem % 2

    def hub_mem(which):
        return 2 * (mid - which)

    def mirrored(which, one_chip):
        return which * (chips - 1) + (1 - 2 * which) * one_chip

    def base_and_slot(which, seen, c):
        first = which * (c // 2) * c
        per_chip = HALF * (1 - which) + which * (2 - c // 2)
        cc = c - first
        near = per_chip + cc * mid + jnp.where(seen < mid, 0, seen - mid)
        far = per_chip + per_chip * mid + cc * (mid - 1) + seen
        place = jnp.where(seen == mid, cc, jnp.where(seen < mid - 1, far, near))
        return first * chips, first * chips + place

    is_hub0 = mem == hub_mem(0)
    is_hub1 = mem == hub_mem(1)
    is_hub = jnp.logical_or(is_hub0, is_hub1)
    role = jnp.where(is_hub1, 1, 0)
    hubs = 2 * groups

    barrier = pltpu.get_barrier_semaphore()

    @pl.when(is_hub)
    def _():
        def greet(k, _):
            pl.semaphore_signal(
                barrier, inc=1, device_id=(clu, (mem + k) % members), device_id_type=MESH
            )
            return 0

        lax.fori_loop(1, members, greet, 0)

        def greet_hub(k, _):
            other = (clu + k) % groups
            for which in (0, 1):
                pl.semaphore_signal(
                    barrier, inc=1, device_id=(other, hub_mem(which)), device_id_type=MESH
                )
            return 0

        lax.fori_loop(1, groups, greet_hub, 0)

    @pl.when(jnp.logical_not(is_hub))
    def _():
        for which in (0, 1):
            pl.semaphore_signal(
                barrier, inc=1, device_id=(clu, hub_mem(which)), device_id_type=MESH
            )

    for s in range(PER):
        mine[s] = emb_ref[order_ref[0, mem * PER + s]]

    def share(which, c):
        _, slot = base_and_slot(which, mirrored(which, chip), c)
        return pltpu.make_async_remote_copy(
            src_ref=mine.at[which * HALF + c],
            dst_ref=buf.at[slot, pl.ds(pl.multiple_of(core * BLK, BLK), BLK)],
            send_sem=send_sem.at[which, c],
            recv_sem=recv_sem.at[slot, core],
            device_id=(clu, hub_mem(which)),
            device_id_type=MESH,
        )

    @pl.when(jnp.logical_not(is_hub))
    def _():
        pl.semaphore_wait(barrier, 2)
        first = jnp.where(chip < mid, 1, 0)

        def step(k, _):
            @pl.when(k < PER)
            def _():
                turn = k // HALF
                share(first * (1 - turn) + (1 - first) * turn, k % HALF).start()

            @pl.when(k >= 2)
            def _():
                done = k - 2
                turn = done // HALF
                share(first * (1 - turn) + (1 - first) * turn, done % HALF).wait_send()

            return 0

        lax.fori_loop(0, PER + 2, step, 0)

    @pl.when(is_hub)
    def _():
        pl.semaphore_wait(barrier, members - 1 + hubs - 2)
        for c in range(HALF):
            share(1 - role, c).start()
        for c in range(HALF):
            _, slot = base_and_slot(role, mid, c)
            buf[slot, :BLK] = mine[role * HALF + c]
        result[...] = jnp.zeros_like(result)

        def event(e, _):
            i = e - HALF
            j = i - HALF * mid
            idx = i % mid
            near = jnp.where(idx == 0, mid - 1, mid + idx)
            seen = jnp.where(i < 0, mid, jnp.where(j < 0, near, j % (mid - 1)))
            c = jnp.where(i < 0, e, jnp.where(j < 0, i // mid, j // (mid - 1)))
            base, slot = base_and_slot(role, seen, c)

            def arrived(half):
                pltpu.make_async_remote_copy(
                    src_ref=mine.at[0],
                    dst_ref=buf.at[slot, pl.ds(half * BLK, BLK)],
                    send_sem=send_sem.at[0, 0],
                    recv_sem=recv_sem.at[slot, half],
                    device_id=(clu, hub_mem(0)),
                    device_id_type=MESH,
                ).wait_recv()

            @pl.when(e >= HALF)
            def _():
                arrived(0)

            arrived(1)
            new = buf[slot]
            wide = new.astype(jnp.float32)
            square = wide * wide
            part = square[:, :BLK]
            for k in range(1, square.shape[1] // BLK):
                part = part + square[:, k * BLK : (k + 1) * BLK]
            hcol[slot] = jnp.broadcast_to(
                0.5 * jnp.sum(part, axis=1, keepdims=True), (UNIT, BLK)
            )
            hrow = 0.5 * jnp.sum(part.T, axis=0, keepdims=True)
            rowacc[slot] = jnp.zeros((UNIT, BLK), jnp.float32)

            def tile(q, carry):
                left, right = carry
                prod = lax.dot_general(
                    buf[q], buf[slot], (((1,), (1,)), ((), ())),
                    preferred_element_type=jnp.float32,
                )
                h = hcol[q]
                t0 = jnp.exp(prod[:, :BLK] - h - hrow[:, :BLK])
                t1 = jnp.exp(prod[:, BLK:] - h - hrow[:, BLK:])
                rowacc[q] += t0 + t1
                left = left + jnp.sum(t0.reshape(UNIT // 8, 8, BLK), axis=0)
                right = right + jnp.sum(t1.reshape(UNIT // 8, 8, BLK), axis=0)
                return left, right

            zero = jnp.zeros((8, BLK), jnp.float32)
            left, right = lax.fori_loop(base, slot + 1, tile, (zero, zero))
            colacc[slot, 0] = left
            colacc[slot, 1] = right
            rowacc[slot] = jnp.zeros((UNIT, BLK), jnp.float32)
            return 0

        lax.fori_loop(0, HALF * chips, event, 0)

        def finish(seen, _):
            holder = mirrored(role, seen)
            for c in range(HALF):
                _, slot = base_and_slot(role, seen, c)
                across = jnp.sum(rowacc[slot].T, axis=0, keepdims=True)
                for half in (0, 1):
                    density = across[:, half * BLK : (half + 1) * BLK] + jnp.sum(
                        colacc[slot, half], axis=0, keepdims=True
                    )
                    result[2 * holder + half, c : c + 1] = 1.0 / density
            return 0

        lax.fori_loop(0, chips, finish, 0)
        own = jnp.sum(result[...], axis=0)
        here = 2 * clu + role
        sums[here] = own

        def sum_copy(k, slot):
            other = (here + k) % hubs
            return pltpu.make_async_remote_copy(
                src_ref=sums.at[here],
                dst_ref=sums.at[slot],
                send_sem=sum_send.at[k],
                recv_sem=sum_recv.at[slot],
                device_id=(other // 2, hub_mem(other % 2)),
                device_id_type=MESH,
            )

        for k in range(1, hubs):
            sum_copy(k, here).start()
        for k in range(1, hubs):
            sum_copy(k, (here + k) % hubs).wait_recv()
        total = jnp.sum(jnp.sum(sums[...], axis=0), keepdims=True)
        rows = float(groups * members * PER * BLK)
        result[...] = result[...] * (rows / total)[None]

        def back(k):
            other = (mem + k) % members
            return pltpu.make_async_remote_copy(
                src_ref=result.at[other],
                dst_ref=weights.at[role],
                send_sem=back_send.at[k],
                recv_sem=back_recv.at[role],
                device_id=(clu, other),
                device_id_type=MESH,
            )

        for k in range(1, members):
            back(k).start()
        weights[role] = result[mem]
        for c in range(HALF):
            share(1 - role, c).wait_send()
        for k in range(1, hubs):
            sum_copy(k, here).wait_send()
        for k in range(1, members):
            back(k).wait_send()

    def returned(which):
        pltpu.make_async_remote_copy(
            src_ref=result.at[0],
            dst_ref=weights.at[which],
            send_sem=back_send.at[0],
            recv_sem=back_recv.at[which],
            device_id=(clu, hub_mem(which)),
            device_id_type=MESH,
        ).wait_recv()

    for which in (0, 1):
        @pl.when(mem != hub_mem(which))
        def _(which=which):
            returned(which)

    for block in range(PER):
        spot = 0
        for s in range(PER):
            spot = jnp.where(order_ref[0, mem * PER + s] == block, s, spot)
        out_ref[block : block + 1] = weights[spot // HALF, pl.ds(spot % HALF, 1)]


def solution(mesh):
    groups, members = mesh.shape["clu"], mesh.shape["mem"]

    def shards(embeddings, block_order):
        rows, width = embeddings.shape
        units = HALF * members // 2
        out = pl.pallas_call(
            functools.partial(kernel, groups, members),
            out_shape=jax.ShapeDtypeStruct((PER, BLK), jnp.float32),
            in_specs=[
                pl.BlockSpec(memory_space=pltpu.SMEM),
                pl.BlockSpec(memory_space=pltpu.VMEM),
            ],
            out_specs=pl.BlockSpec(memory_space=pltpu.VMEM),
            scratch_shapes=[
                pltpu.VMEM((PER, BLK, width), jnp.bfloat16),
                pltpu.VMEM((units, UNIT, width), jnp.bfloat16),
                pltpu.VMEM((units, UNIT, BLK), jnp.float32),
                pltpu.VMEM((units, 2, 8, BLK), jnp.float32),
                pltpu.VMEM((units, UNIT, BLK), jnp.float32),
                pltpu.VMEM((members, 8, BLK), jnp.float32),
                pltpu.VMEM((2 * groups, 8, BLK), jnp.float32),
                pltpu.VMEM((2, 8, BLK), jnp.float32),
                pltpu.SemaphoreType.DMA((2, HALF)),
                pltpu.SemaphoreType.DMA((units, 2)),
                pltpu.SemaphoreType.DMA((2 * groups,)),
                pltpu.SemaphoreType.DMA((2 * groups,)),
                pltpu.SemaphoreType.DMA((members,)),
                pltpu.SemaphoreType.DMA((2,)),
            ],
            compiler_params=pltpu.CompilerParams(
                collective_id=0, has_side_effects=True, vmem_limit_bytes=48 * 1024 * 1024
            ),
            cost_estimate=pl.CostEstimate(
                flops=2 * rows * rows * members * width // 6,
                bytes_accessed=rows * width * 2,
                transcendentals=rows * rows,
            ),
        )(block_order, embeddings.reshape(PER, BLK, width))
        return out.reshape(rows)

    return jax.shard_map(
        shards,
        mesh=mesh,
        in_specs=(P(("clu", "mem"), None), P("clu", None)),
        out_specs=P(("clu", "mem")),
        check_vma=False,
    )
```

```python
import functools

import jax
import jax.numpy as jnp
from jax import lax
from jax.experimental import pallas as pl
from jax.experimental.pallas import tpu as pltpu
from jax.sharding import PartitionSpec as P

BLK = 128
PER = 8
HALF = PER // 2
UNIT = 2 * BLK
MESH = pl.DeviceIdType.MESH


def kernel(
    groups, members, order_hbm, emb_hbm, out_ref,
    order_ref, emb_ref, load_sem, mine, buf, rowacc, colacc, hcol, result, sums, weights,
    send_sem, recv_sem, sum_send, sum_recv, back_send, back_recv,
):
    chips = members // 2
    mid = chips // 2
    clu = lax.axis_index("clu")
    mem = lax.axis_index("mem")
    chip, core = mem // 2, mem % 2

    def hub_mem(which):
        return 2 * (mid - which)

    def mirrored(which, one_chip):
        return which * (chips - 1) + (1 - 2 * which) * one_chip

    def base_and_slot(which, seen, c):
        first = which * (c // 2) * c
        per_chip = HALF * (1 - which) + which * (2 - c // 2)
        cc = c - first
        near = per_chip + cc * mid + jnp.where(seen < mid, 0, seen - mid)
        far = per_chip + per_chip * mid + cc * (mid - 1) + seen
        place = jnp.where(seen == mid, cc, jnp.where(seen < mid - 1, far, near))
        return first * chips, first * chips + place

    is_hub0 = mem == hub_mem(0)
    is_hub1 = mem == hub_mem(1)
    is_hub = jnp.logical_or(is_hub0, is_hub1)
    role = jnp.where(is_hub1, 1, 0)
    hubs = 2 * groups

    load_order = pltpu.make_async_copy(order_hbm, order_ref, load_sem.at[0])
    load_emb = pltpu.make_async_copy(emb_hbm, emb_ref, load_sem.at[1])
    load_order.start()
    load_emb.start()
    barrier = pltpu.get_barrier_semaphore()

    @pl.when(is_hub)
    def _():
        def greet(k, _):
            pl.semaphore_signal(
                barrier, inc=1, device_id=(clu, (mem + k) % members), device_id_type=MESH
            )
            return 0

        lax.fori_loop(1, members, greet, 0)

        def greet_hub(k, _):
            other = (clu + k) % groups
            for which in (0, 1):
                pl.semaphore_signal(
                    barrier, inc=1, device_id=(other, hub_mem(which)), device_id_type=MESH
                )
            return 0

        lax.fori_loop(1, groups, greet_hub, 0)

    @pl.when(jnp.logical_not(is_hub))
    def _():
        for which in (0, 1):
            pl.semaphore_signal(
                barrier, inc=1, device_id=(clu, hub_mem(which)), device_id_type=MESH
            )

    load_order.wait()
    load_emb.wait()
    for s in range(PER):
        mine[s] = emb_ref[order_ref[0, mem * PER + s]]

    def share(which, c):
        _, slot = base_and_slot(which, mirrored(which, chip), c)
        return pltpu.make_async_remote_copy(
            src_ref=mine.at[which * HALF + c],
            dst_ref=buf.at[slot, pl.ds(pl.multiple_of(core * BLK, BLK), BLK)],
            send_sem=send_sem.at[which, c],
            recv_sem=recv_sem.at[slot, core],
            device_id=(clu, hub_mem(which)),
            device_id_type=MESH,
        )

    @pl.when(jnp.logical_not(is_hub))
    def _():
        pl.semaphore_wait(barrier, 2)
        first = jnp.where(chip < mid, 1, 0)

        def step(k, _):
            @pl.when(k < PER)
            def _():
                turn = k // HALF
                share(first * (1 - turn) + (1 - first) * turn, k % HALF).start()

            @pl.when(k >= 2)
            def _():
                done = k - 2
                turn = done // HALF
                share(first * (1 - turn) + (1 - first) * turn, done % HALF).wait_send()

            return 0

        lax.fori_loop(0, PER + 2, step, 0)

    @pl.when(is_hub)
    def _():
        pl.semaphore_wait(barrier, members - 1 + hubs - 2)
        for c in range(HALF):
            share(1 - role, c).start()
        for c in range(HALF):
            _, slot = base_and_slot(role, mid, c)
            buf[slot, :BLK] = mine[role * HALF + c]
        result[...] = jnp.zeros_like(result)

        def event(e, _):
            i = e - HALF
            j = i - HALF * mid
            idx = i % mid
            near = jnp.where(idx == 0, mid - 1, mid + idx)
            seen = jnp.where(i < 0, mid, jnp.where(j < 0, near, j % (mid - 1)))
            c = jnp.where(i < 0, e, jnp.where(j < 0, i // mid, j // (mid - 1)))
            base, slot = base_and_slot(role, seen, c)

            def arrived(half):
                pltpu.make_async_remote_copy(
                    src_ref=mine.at[0],
                    dst_ref=buf.at[slot, pl.ds(half * BLK, BLK)],
                    send_sem=send_sem.at[0, 0],
                    recv_sem=recv_sem.at[slot, half],
                    device_id=(clu, hub_mem(0)),
                    device_id_type=MESH,
                ).wait_recv()

            @pl.when(e >= HALF)
            def _():
                arrived(0)

            arrived(1)
            new = buf[slot]
            wide = new.astype(jnp.float32)
            square = wide * wide
            part = square[:, :BLK]
            for k in range(1, square.shape[1] // BLK):
                part = part + square[:, k * BLK : (k + 1) * BLK]
            hcol[slot] = jnp.broadcast_to(
                0.5 * jnp.sum(part, axis=1, keepdims=True), (UNIT, BLK)
            )
            hrow = 0.5 * jnp.sum(part.T, axis=0, keepdims=True)
            rowacc[slot] = jnp.zeros((UNIT, BLK), jnp.float32)

            colacc[slot] = jnp.zeros((2, 8, BLK), jnp.float32)

            def tiles(q, count):
                for k in range(count):
                    prod = lax.dot_general(
                        buf[q + k], buf[slot], (((1,), (1,)), ((), ())),
                        preferred_element_type=jnp.float32,
                    )
                    h = hcol[q + k]
                    t0 = jnp.exp(prod[:, :BLK] - h - hrow[:, :BLK])
                    t1 = jnp.exp(prod[:, BLK:] - h - hrow[:, BLK:])
                    rowacc[q + k] += t0 + t1
                    colacc[slot, 0] += jnp.sum(t0.reshape(UNIT // 8, 8, BLK), axis=0)
                    colacc[slot, 1] += jnp.sum(t1.reshape(UNIT // 8, 8, BLK), axis=0)

            count = slot + 1 - base
            quads = count // 4

            def four(k, _):
                tiles(base + 4 * k, 4)
                return 0

            lax.fori_loop(0, quads, four, 0)
            rest = base + 4 * quads

            @pl.when(count % 4 >= 2)
            def _():
                tiles(rest, 2)

            @pl.when(count % 2 == 1)
            def _():
                tiles(slot, 1)

            rowacc[slot] = jnp.zeros((UNIT, BLK), jnp.float32)
            return 0

        lax.fori_loop(0, HALF * chips, event, 0)

        def finish(seen, _):
            holder = mirrored(role, seen)
            for c in range(HALF):
                _, slot = base_and_slot(role, seen, c)
                across = jnp.sum(rowacc[slot].T, axis=0, keepdims=True)
                for half in (0, 1):
                    density = across[:, half * BLK : (half + 1) * BLK] + jnp.sum(
                        colacc[slot, half], axis=0, keepdims=True
                    )
                    result[2 * holder + half, c : c + 1] = 1.0 / density
            return 0

        lax.fori_loop(0, chips, finish, 0)
        own = jnp.sum(result[...], axis=0)
        here = 2 * clu + role
        sums[here] = own

        def sum_copy(k, slot):
            other = (here + k) % hubs
            return pltpu.make_async_remote_copy(
                src_ref=sums.at[here],
                dst_ref=sums.at[slot],
                send_sem=sum_send.at[k],
                recv_sem=sum_recv.at[slot],
                device_id=(other // 2, hub_mem(other % 2)),
                device_id_type=MESH,
            )

        for k in range(1, hubs):
            sum_copy(k, here).start()
        for k in range(1, hubs):
            sum_copy(k, (here + k) % hubs).wait_recv()
        total = jnp.sum(jnp.sum(sums[...], axis=0), keepdims=True)
        rows = float(groups * members * PER * BLK)
        result[...] = result[...] * (rows / total)[None]

        def back(k):
            other = (mem + k) % members
            return pltpu.make_async_remote_copy(
                src_ref=result.at[other],
                dst_ref=weights.at[role],
                send_sem=back_send.at[k],
                recv_sem=back_recv.at[role],
                device_id=(clu, other),
                device_id_type=MESH,
            )

        for k in range(1, members):
            back(k).start()
        weights[role] = result[mem]
        for c in range(HALF):
            share(1 - role, c).wait_send()
        for k in range(1, hubs):
            sum_copy(k, here).wait_send()
        for k in range(1, members):
            back(k).wait_send()

    def returned(which):
        pltpu.make_async_remote_copy(
            src_ref=result.at[0],
            dst_ref=weights.at[which],
            send_sem=back_send.at[0],
            recv_sem=back_recv.at[which],
            device_id=(clu, hub_mem(which)),
            device_id_type=MESH,
        ).wait_recv()

    for which in (0, 1):
        @pl.when(mem != hub_mem(which))
        def _(which=which):
            returned(which)

    for block in range(PER):
        spot = 0
        for s in range(PER):
            spot = jnp.where(order_ref[0, mem * PER + s] == block, s, spot)
        out_ref[block : block + 1] = weights[spot // HALF, pl.ds(spot % HALF, 1)]


def solution(mesh):
    groups, members = mesh.shape["clu"], mesh.shape["mem"]

    def shards(embeddings, block_order):
        rows, width = embeddings.shape
        units = HALF * members // 2
        out = pl.pallas_call(
            functools.partial(kernel, groups, members),
            out_shape=jax.ShapeDtypeStruct((PER, BLK), jnp.float32),
            in_specs=[pl.BlockSpec(memory_space=pl.ANY)] * 2,
            out_specs=pl.BlockSpec(memory_space=pltpu.VMEM),
            scratch_shapes=[
                pltpu.SMEM(block_order.shape, jnp.int32),
                pltpu.VMEM((PER, BLK, width), jnp.bfloat16),
                pltpu.SemaphoreType.DMA((2,)),
                pltpu.VMEM((PER, BLK, width), jnp.bfloat16),
                pltpu.VMEM((units, UNIT, width), jnp.bfloat16),
                pltpu.VMEM((units, UNIT, BLK), jnp.float32),
                pltpu.VMEM((units, 2, 8, BLK), jnp.float32),
                pltpu.VMEM((units, UNIT, BLK), jnp.float32),
                pltpu.VMEM((members, 8, BLK), jnp.float32),
                pltpu.VMEM((2 * groups, 8, BLK), jnp.float32),
                pltpu.VMEM((2, 8, BLK), jnp.float32),
                pltpu.SemaphoreType.DMA((2, HALF)),
                pltpu.SemaphoreType.DMA((units, 2)),
                pltpu.SemaphoreType.DMA((2 * groups,)),
                pltpu.SemaphoreType.DMA((2 * groups,)),
                pltpu.SemaphoreType.DMA((members,)),
                pltpu.SemaphoreType.DMA((2,)),
            ],
            compiler_params=pltpu.CompilerParams(
                collective_id=0, has_side_effects=True, vmem_limit_bytes=48 * 1024 * 1024
            ),
            cost_estimate=pl.CostEstimate(
                flops=2 * rows * rows * members * width // 6,
                bytes_accessed=rows * width * 2,
                transcendentals=rows * rows,
            ),
        )(block_order, embeddings.reshape(PER, BLK, width))
        return out.reshape(rows)

    return jax.shard_map(
        shards,
        mesh=mesh,
        in_specs=(P(("clu", "mem"), None), P("clu", None)),
        out_specs=P(("clu", "mem")),
        check_vma=False,
    )
```

```python
import functools

import jax
import jax.numpy as jnp
from jax import lax
from jax.experimental import pallas as pl
from jax.experimental.pallas import tpu as pltpu
from jax.sharding import PartitionSpec as P

BLK = 128
PER = 8
HALF = PER // 2
UNIT = 2 * BLK
MESH = pl.DeviceIdType.MESH


def kernel(
    groups, members, order_hbm, emb_hbm, out_ref,
    order_ref, emb_ref, load_sem, mine, buf, rowacc, colacc, hcol, result, sums, weights,
    partial, send_sem, recv_sem, pass_send, pass_recv, part_sem, sum_send, sum_recv, back_send, back_recv,
):
    chips = members // 2
    mid = chips // 2
    clu = lax.axis_index("clu")
    mem = lax.axis_index("mem")
    chip, core = mem // 2, mem % 2

    def hub_mem(which):
        return 2 * (mid - which)

    def mirrored(which, one_chip):
        return which * (chips - 1) + (1 - 2 * which) * one_chip

    def base_and_slot(which, seen, c):
        first = which * (c // 2) * c
        per_chip = HALF * (1 - which) + which * (2 - c // 2)
        cc = c - first
        near = per_chip + cc * mid + jnp.where(seen < mid, 0, seen - mid)
        far = per_chip + per_chip * mid + cc * (mid - 1) + seen
        place = jnp.where(seen == mid, cc, jnp.where(seen < mid - 1, far, near))
        return first * chips, first * chips + place

    hub_chip = jnp.logical_or(chip == mid, chip == mid - 1)
    is_hub = jnp.logical_and(hub_chip, core == 0)
    is_near = jnp.logical_and(hub_chip, core == 1)
    role = jnp.where(chip == mid - 1, 1, 0)
    hubs = 2 * groups
    events = HALF * chips
    near_events = HALF + HALF * mid

    load_order = pltpu.make_async_copy(order_hbm, order_ref, load_sem.at[0])
    load_emb = pltpu.make_async_copy(emb_hbm, emb_ref, load_sem.at[1])
    load_order.start()
    load_emb.start()
    barrier = pltpu.get_barrier_semaphore()

    @pl.when(hub_chip)
    def _():
        def greet(k, _):
            pl.semaphore_signal(
                barrier, inc=1, device_id=(clu, (mem + k) % members), device_id_type=MESH
            )
            return 0

        lax.fori_loop(1, members, greet, 0)

    @pl.when(is_hub)
    def _():
        def greet_hub(k, _):
            other = (clu + k) % groups
            for which in (0, 1):
                pl.semaphore_signal(
                    barrier, inc=1, device_id=(other, hub_mem(which)), device_id_type=MESH
                )
            return 0

        lax.fori_loop(1, groups, greet_hub, 0)

    @pl.when(jnp.logical_not(hub_chip))
    def _():
        for which in (0, 1):
            for half in (0, 1):
                pl.semaphore_signal(
                    barrier, inc=1, device_id=(clu, hub_mem(which) + half),
                    device_id_type=MESH,
                )

    load_order.wait()
    load_emb.wait()
    for s in range(PER):
        mine[s] = emb_ref[order_ref[0, mem * PER + s]]

    def share(which, c):
        seen = mirrored(which, chip)
        _, slot = base_and_slot(which, seen, c)
        return pltpu.make_async_remote_copy(
            src_ref=mine.at[which * HALF + c],
            dst_ref=buf.at[slot, pl.ds(pl.multiple_of(core * BLK, BLK), BLK)],
            send_sem=send_sem.at[which, c],
            recv_sem=recv_sem.at[slot, core],
            device_id=(clu, hub_mem(which) + jnp.where(seen < mid - 1, 0, 1)),
            device_id_type=MESH,
        )

    def at_event(e):
        i = e - HALF
        j = i - HALF * mid
        idx = i % mid
        near = jnp.where(idx == 0, mid - 1, mid + idx)
        seen = jnp.where(i < 0, mid, jnp.where(j < 0, near, j % (mid - 1)))
        c = jnp.where(i < 0, e, jnp.where(j < 0, i // mid, j // (mid - 1)))
        return base_and_slot(role, seen, c)

    def arrived(slot, half):
        pltpu.make_async_remote_copy(
            src_ref=mine.at[0],
            dst_ref=buf.at[slot, pl.ds(half * BLK, BLK)],
            send_sem=send_sem.at[0, 0],
            recv_sem=recv_sem.at[slot, half],
            device_id=(clu, hub_mem(0)),
            device_id_type=MESH,
        ).wait_recv()

    def passed(slot):
        return pltpu.make_async_remote_copy(
            src_ref=buf.at[slot],
            dst_ref=buf.at[slot],
            send_sem=pass_send.at[slot],
            recv_sem=pass_recv.at[slot],
            device_id=(clu, 2 * chip),
            device_id_type=MESH,
        )

    part_copy = pltpu.make_async_remote_copy(
        src_ref=partial,
        dst_ref=partial,
        send_sem=part_sem.at[0],
        recv_sem=part_sem.at[1],
        device_id=(clu, 2 * chip),
        device_id_type=MESH,
    )

    def norms(slot):
        wide = buf[slot].astype(jnp.float32)
        square = wide * wide
        part = square[:, :BLK]
        for k in range(1, square.shape[1] // BLK):
            part = part + square[:, k * BLK : (k + 1) * BLK]
        hcol[slot] = jnp.broadcast_to(
            0.5 * jnp.sum(part, axis=1, keepdims=True), (UNIT, BLK)
        )
        rowacc[slot] = jnp.zeros((UNIT, BLK), jnp.float32)
        colacc[slot] = jnp.zeros((2, 8, BLK), jnp.float32)
        return 0.5 * jnp.sum(part.T, axis=0, keepdims=True)

    def compare(base, slot, hrow):
        def tiles(q, count):
            for k in range(count):
                prod = lax.dot_general(
                    buf[q + k], buf[slot], (((1,), (1,)), ((), ())),
                    preferred_element_type=jnp.float32,
                )
                h = hcol[q + k]
                t0 = jnp.exp(prod[:, :BLK] - h - hrow[:, :BLK])
                t1 = jnp.exp(prod[:, BLK:] - h - hrow[:, BLK:])
                rowacc[q + k] += t0 + t1
                colacc[slot, 0] += jnp.sum(t0.reshape(UNIT // 8, 8, BLK), axis=0)
                colacc[slot, 1] += jnp.sum(t1.reshape(UNIT // 8, 8, BLK), axis=0)

        count = slot + 1 - base
        quads = count // 4

        def four(k, _):
            tiles(base + 4 * k, 4)
            return 0

        lax.fori_loop(0, quads, four, 0)

        @pl.when(count % 4 >= 2)
        def _():
            tiles(base + 4 * quads, 2)

        @pl.when(count % 2 == 1)
        def _():
            tiles(slot, 1)

        rowacc[slot] = jnp.zeros((UNIT, BLK), jnp.float32)

    def density(slot):
        across = jnp.sum(rowacc[slot].T, axis=0, keepdims=True)
        down = jnp.sum(colacc[slot], axis=1)
        return across + jnp.concatenate([down[:1], down[1:]], axis=1)

    @pl.when(jnp.logical_not(hub_chip))
    def _():
        pl.semaphore_wait(barrier, 4)
        first = jnp.where(chip < mid, 1, 0)

        def step(k, _):
            @pl.when(k < PER)
            def _():
                turn = k // HALF
                share(first * (1 - turn) + (1 - first) * turn, k % HALF).start()

            @pl.when(k >= 2)
            def _():
                done = k - 2
                turn = done // HALF
                share(first * (1 - turn) + (1 - first) * turn, done % HALF).wait_send()

            return 0

        lax.fori_loop(0, PER + 2, step, 0)

    @pl.when(is_near)
    def _():
        pl.semaphore_wait(barrier, members - 1)
        for c in range(HALF):
            share(1 - role, c).start()
        for c in range(HALF):
            _, slot = base_and_slot(role, mid, c)
            buf[slot, BLK:] = mine[role * HALF + c]
        partial[...] = jnp.zeros_like(partial)

        def event(e, _):
            base, slot = at_event(e)
            arrived(slot, 0)

            @pl.when(e >= HALF)
            def _():
                arrived(slot, 1)

            passed(slot).start()
            compare(base, slot, norms(slot))
            return 0

        lax.fori_loop(0, near_events, event, 0)

        def fill(e, _):
            _, slot = at_event(e)
            partial[pl.ds(slot, 1)] = density(slot)
            return 0

        lax.fori_loop(0, near_events, fill, 0)
        part_copy.start()

        def drain(e, _):
            _, slot = at_event(e)
            passed(slot).wait_send()
            return 0

        lax.fori_loop(0, near_events, drain, 0)
        for c in range(HALF):
            share(1 - role, c).wait_send()
        part_copy.wait_send()

    @pl.when(is_hub)
    def _():
        pl.semaphore_wait(barrier, members - 1 + hubs - 2)
        for c in range(HALF):
            share(role, c).start()
        for c in range(HALF):
            share(1 - role, c).start()
        result[...] = jnp.zeros_like(result)

        def take(e, _):
            _, slot = at_event(e)
            passed(slot).wait_recv()
            norms(slot)
            return 0

        lax.fori_loop(0, near_events, take, 0)

        def event(e, _):
            base, slot = at_event(e)
            arrived(slot, 0)
            arrived(slot, 1)
            compare(base, slot, norms(slot))
            return 0

        lax.fori_loop(near_events, events, event, 0)
        part_copy.wait_recv()

        def finish(seen, _):
            holder = mirrored(role, seen)
            for c in range(HALF):
                _, slot = base_and_slot(role, seen, c)
                inverse = 1.0 / (density(slot) + partial[pl.ds(slot, 1)])
                for half in (0, 1):
                    result[2 * holder + half, c : c + 1] = inverse[
                        :, half * BLK : (half + 1) * BLK
                    ]
            return 0

        lax.fori_loop(0, chips, finish, 0)
        own = jnp.sum(result[...], axis=0)
        here = 2 * clu + role
        sums[here] = own

        def sum_copy(k, slot):
            other = (here + k) % hubs
            return pltpu.make_async_remote_copy(
                src_ref=sums.at[here],
                dst_ref=sums.at[slot],
                send_sem=sum_send.at[k],
                recv_sem=sum_recv.at[slot],
                device_id=(other // 2, hub_mem(other % 2)),
                device_id_type=MESH,
            )

        for k in range(1, hubs):
            sum_copy(k, here).start()
        for k in range(1, hubs):
            sum_copy(k, (here + k) % hubs).wait_recv()
        total = jnp.sum(jnp.sum(sums[...], axis=0), keepdims=True)
        rows = float(groups * members * PER * BLK)
        result[...] = result[...] * (rows / total)[None]

        def back(k):
            other = (mem + k) % members
            return pltpu.make_async_remote_copy(
                src_ref=result.at[other],
                dst_ref=weights.at[role],
                send_sem=back_send.at[k],
                recv_sem=back_recv.at[role],
                device_id=(clu, other),
                device_id_type=MESH,
            )

        for k in range(1, members):
            back(k).start()
        weights[role] = result[mem]
        for c in range(HALF):
            share(role, c).wait_send()
            share(1 - role, c).wait_send()
        for k in range(1, hubs):
            sum_copy(k, here).wait_send()
        for k in range(1, members):
            back(k).wait_send()

    def returned(which):
        pltpu.make_async_remote_copy(
            src_ref=result.at[0],
            dst_ref=weights.at[which],
            send_sem=back_send.at[0],
            recv_sem=back_recv.at[which],
            device_id=(clu, hub_mem(which)),
            device_id_type=MESH,
        ).wait_recv()

    for which in (0, 1):
        @pl.when(mem != hub_mem(which))
        def _(which=which):
            returned(which)

    for block in range(PER):
        spot = 0
        for s in range(PER):
            spot = jnp.where(order_ref[0, mem * PER + s] == block, s, spot)
        out_ref[block : block + 1] = weights[spot // HALF, pl.ds(spot % HALF, 1)]


def solution(mesh):
    groups, members = mesh.shape["clu"], mesh.shape["mem"]

    def shards(embeddings, block_order):
        rows, width = embeddings.shape
        units = HALF * members // 2
        out = pl.pallas_call(
            functools.partial(kernel, groups, members),
            out_shape=jax.ShapeDtypeStruct((PER, BLK), jnp.float32),
            in_specs=[pl.BlockSpec(memory_space=pl.ANY)] * 2,
            out_specs=pl.BlockSpec(memory_space=pltpu.VMEM),
            scratch_shapes=[
                pltpu.SMEM(block_order.shape, jnp.int32),
                pltpu.VMEM((PER, BLK, width), jnp.bfloat16),
                pltpu.SemaphoreType.DMA((2,)),
                pltpu.VMEM((PER, BLK, width), jnp.bfloat16),
                pltpu.VMEM((units, UNIT, width), jnp.bfloat16),
                pltpu.VMEM((units, UNIT, BLK), jnp.float32),
                pltpu.VMEM((units, 2, 8, BLK), jnp.float32),
                pltpu.VMEM((units, UNIT, BLK), jnp.float32),
                pltpu.VMEM((members, 8, BLK), jnp.float32),
                pltpu.VMEM((2 * groups, 8, BLK), jnp.float32),
                pltpu.VMEM((2, 8, BLK), jnp.float32),
                pltpu.VMEM((units, UNIT), jnp.float32),
                pltpu.SemaphoreType.DMA((2, HALF)),
                pltpu.SemaphoreType.DMA((units, 2)),
                pltpu.SemaphoreType.DMA((units,)),
                pltpu.SemaphoreType.DMA((units,)),
                pltpu.SemaphoreType.DMA((2,)),
                pltpu.SemaphoreType.DMA((2 * groups,)),
                pltpu.SemaphoreType.DMA((2 * groups,)),
                pltpu.SemaphoreType.DMA((members,)),
                pltpu.SemaphoreType.DMA((2,)),
            ],
            compiler_params=pltpu.CompilerParams(
                collective_id=0, has_side_effects=True, vmem_limit_bytes=60 * 1024 * 1024
            ),
            cost_estimate=pl.CostEstimate(
                flops=2 * rows * rows * members * width // 6,
                bytes_accessed=rows * width * 2,
                transcendentals=rows * rows,
            ),
        )(block_order, embeddings.reshape(PER, BLK, width))
        return out.reshape(rows)

    return jax.shard_map(
        shards,
        mesh=mesh,
        in_specs=(P(("clu", "mem"), None), P("clu", None)),
        out_specs=P(("clu", "mem")),
        check_vma=False,
    )
```

```python
import functools

import jax
import jax.numpy as jnp
from jax import lax
from jax.experimental import pallas as pl
from jax.experimental.pallas import tpu as pltpu
from jax.sharding import PartitionSpec as P

BLK = 128
PER = 8
HALF = PER // 2
UNIT = 2 * BLK
MESH = pl.DeviceIdType.MESH


def kernel(
    groups, members, order_hbm, emb_hbm, out_ref,
    order_ref, emb_ref, load_sem, mine, buf, rowacc, colacc, hcol, result, sums, weights,
    partial, send_sem, recv_sem, pass_send, pass_recv, part_sem, sum_send, sum_recv, back_send, back_recv,
):
    chips = members // 2
    mid = chips // 2
    clu = lax.axis_index("clu")
    mem = lax.axis_index("mem")
    chip, core = mem // 2, mem % 2

    def hub_mem(which):
        return 2 * (mid - which)

    def mirrored(which, one_chip):
        return which * (chips - 1) + (1 - 2 * which) * one_chip

    def base_and_slot(which, seen, c):
        first = which * (c // 2) * c
        per_chip = HALF * (1 - which) + which * (2 - c // 2)
        cc = c - first
        near = per_chip + cc * mid + jnp.where(seen < mid, 0, seen - mid)
        far = per_chip + per_chip * mid + cc * (mid - 1) + seen
        place = jnp.where(seen == mid, cc, jnp.where(seen < mid - 1, far, near))
        return first * chips, first * chips + place

    hub_chip = jnp.logical_or(chip == mid, chip == mid - 1)
    is_hub = jnp.logical_and(hub_chip, core == 0)
    is_near = jnp.logical_and(hub_chip, core == 1)
    role = jnp.where(chip == mid - 1, 1, 0)
    hubs = 2 * groups
    events = HALF * chips
    near_events = HALF + HALF * mid

    load_order = pltpu.make_async_copy(order_hbm, order_ref, load_sem.at[0])
    load_emb = pltpu.make_async_copy(emb_hbm, emb_ref, load_sem.at[1])
    load_order.start()
    load_emb.start()
    barrier = pltpu.get_barrier_semaphore()

    @pl.when(hub_chip)
    def _():
        def greet(k, _):
            pl.semaphore_signal(
                barrier, inc=1, device_id=(clu, (mem + k) % members), device_id_type=MESH
            )
            return 0

        lax.fori_loop(1, members, greet, 0)

    @pl.when(is_hub)
    def _():
        def greet_hub(k, _):
            other = (clu + k) % groups
            for which in (0, 1):
                pl.semaphore_signal(
                    barrier, inc=1, device_id=(other, hub_mem(which)), device_id_type=MESH
                )
            return 0

        lax.fori_loop(1, groups, greet_hub, 0)

    @pl.when(jnp.logical_not(hub_chip))
    def _():
        for which in (0, 1):
            for half in (0, 1):
                pl.semaphore_signal(
                    barrier, inc=1, device_id=(clu, hub_mem(which) + half),
                    device_id_type=MESH,
                )

    load_order.wait()
    load_emb.wait()
    for s in range(PER):
        mine[s] = emb_ref[order_ref[0, mem * PER + s]]

    def share(which, c):
        seen = mirrored(which, chip)
        _, slot = base_and_slot(which, seen, c)
        return pltpu.make_async_remote_copy(
            src_ref=mine.at[which * HALF + c],
            dst_ref=buf.at[slot, pl.ds(pl.multiple_of(core * BLK, BLK), BLK)],
            send_sem=send_sem.at[which, c],
            recv_sem=recv_sem.at[slot, core],
            device_id=(clu, hub_mem(which) + jnp.where(seen < mid - 1, 0, 1)),
            device_id_type=MESH,
        )

    def at_event(e):
        i = e - HALF
        j = i - HALF * mid
        idx = i % mid
        near = jnp.where(idx == 0, mid - 1, mid + idx)
        seen = jnp.where(i < 0, mid, jnp.where(j < 0, near, j % (mid - 1)))
        c = jnp.where(i < 0, e, jnp.where(j < 0, i // mid, j // (mid - 1)))
        return base_and_slot(role, seen, c)

    def arrived(slot, half):
        pltpu.make_async_remote_copy(
            src_ref=mine.at[0],
            dst_ref=buf.at[slot, pl.ds(half * BLK, BLK)],
            send_sem=send_sem.at[0, 0],
            recv_sem=recv_sem.at[slot, half],
            device_id=(clu, hub_mem(0)),
            device_id_type=MESH,
        ).wait_recv()

    def passed(slot):
        return pltpu.make_async_remote_copy(
            src_ref=buf.at[slot],
            dst_ref=buf.at[slot],
            send_sem=pass_send.at[slot],
            recv_sem=pass_recv.at[slot],
            device_id=(clu, 2 * chip),
            device_id_type=MESH,
        )

    part_copy = pltpu.make_async_remote_copy(
        src_ref=partial,
        dst_ref=partial,
        send_sem=part_sem.at[0],
        recv_sem=part_sem.at[1],
        device_id=(clu, 2 * chip),
        device_id_type=MESH,
    )

    def norms(slot):
        wide = buf[slot].astype(jnp.float32)
        square = wide * wide
        part = square[:, :BLK]
        for k in range(1, square.shape[1] // BLK):
            part = part + square[:, k * BLK : (k + 1) * BLK]
        hcol[slot] = jnp.broadcast_to(
            0.5 * jnp.sum(part, axis=1, keepdims=True), (UNIT, BLK)
        )
        rowacc[slot] = jnp.zeros((UNIT, BLK), jnp.float32)
        colacc[slot] = jnp.zeros((2, 8, BLK), jnp.float32)
        return 0.5 * jnp.sum(part.T, axis=0, keepdims=True)

    def compare(base, slot, hrow):
        def tiles(q, count):
            for k in range(count):
                prod = lax.dot_general(
                    buf[q + k], buf[slot], (((1,), (1,)), ((), ())),
                    preferred_element_type=jnp.float32,
                )
                h = hcol[q + k]
                t0 = jnp.exp(prod[:, :BLK] - h - hrow[:, :BLK])
                t1 = jnp.exp(prod[:, BLK:] - h - hrow[:, BLK:])
                rowacc[q + k] += t0 + t1
                colacc[slot, 0] += jnp.sum(t0.reshape(UNIT // 8, 8, BLK), axis=0)
                colacc[slot, 1] += jnp.sum(t1.reshape(UNIT // 8, 8, BLK), axis=0)

        count = slot + 1 - base
        quads = count // 4

        def four(k, _):
            tiles(base + 4 * k, 4)
            return 0

        lax.fori_loop(0, quads, four, 0)

        @pl.when(count % 4 >= 2)
        def _():
            tiles(base + 4 * quads, 2)

        @pl.when(count % 2 == 1)
        def _():
            tiles(slot, 1)

        rowacc[slot] = jnp.zeros((UNIT, BLK), jnp.float32)

    def density(slot):
        across = jnp.sum(rowacc[slot].T, axis=0, keepdims=True)
        down = jnp.sum(colacc[slot], axis=1)
        return across + jnp.concatenate([down[:1], down[1:]], axis=1)

    @pl.when(jnp.logical_not(hub_chip))
    def _():
        pl.semaphore_wait(barrier, 4)
        first = jnp.where(chip < mid, 1, 0)

        def step(k, _):
            @pl.when(k < PER)
            def _():
                turn = k // HALF
                share(first * (1 - turn) + (1 - first) * turn, k % HALF).start()

            @pl.when(k >= HALF)
            def _():
                done = k - HALF
                turn = done // HALF
                share(first * (1 - turn) + (1 - first) * turn, done % HALF).wait_send()

            return 0

        lax.fori_loop(0, PER + HALF, step, 0)

    @pl.when(is_near)
    def _():
        pl.semaphore_wait(barrier, members - 1)
        for c in range(HALF):
            share(1 - role, c).start()
        for c in range(HALF):
            _, slot = base_and_slot(role, mid, c)
            buf[slot, BLK:] = mine[role * HALF + c]
        partial[...] = jnp.zeros_like(partial)

        def event(e, _):
            base, slot = at_event(e)
            arrived(slot, 0)

            @pl.when(e >= HALF)
            def _():
                arrived(slot, 1)

            passed(slot).start()
            compare(base, slot, norms(slot))
            return 0

        lax.fori_loop(0, near_events, event, 0)

        def fill(e, _):
            _, slot = at_event(e)
            partial[pl.ds(slot, 1)] = density(slot)
            return 0

        lax.fori_loop(0, near_events, fill, 0)
        part_copy.start()

        def drain(e, _):
            _, slot = at_event(e)
            passed(slot).wait_send()
            return 0

        lax.fori_loop(0, near_events, drain, 0)
        for c in range(HALF):
            share(1 - role, c).wait_send()
        part_copy.wait_send()

    @pl.when(is_hub)
    def _():
        pl.semaphore_wait(barrier, members - 1 + hubs - 2)
        for c in range(HALF):
            share(role, c).start()
        for c in range(HALF):
            share(1 - role, c).start()
        result[...] = jnp.zeros_like(result)

        def take(e, _):
            _, slot = at_event(e)
            passed(slot).wait_recv()
            norms(slot)
            return 0

        lax.fori_loop(0, near_events, take, 0)

        def event(e, _):
            base, slot = at_event(e)
            arrived(slot, 0)
            arrived(slot, 1)
            compare(base, slot, norms(slot))
            return 0

        lax.fori_loop(near_events, events, event, 0)
        part_copy.wait_recv()

        def finish(seen, _):
            holder = mirrored(role, seen)
            for c in range(HALF):
                _, slot = base_and_slot(role, seen, c)
                inverse = 1.0 / (density(slot) + partial[pl.ds(slot, 1)])
                for half in (0, 1):
                    result[2 * holder + half, c : c + 1] = inverse[
                        :, half * BLK : (half + 1) * BLK
                    ]
            return 0

        lax.fori_loop(0, chips, finish, 0)
        own = jnp.sum(result[...], axis=0)
        here = 2 * clu + role
        sums[here] = own

        def sum_copy(k, slot):
            other = (here + k) % hubs
            return pltpu.make_async_remote_copy(
                src_ref=sums.at[here],
                dst_ref=sums.at[slot],
                send_sem=sum_send.at[k],
                recv_sem=sum_recv.at[slot],
                device_id=(other // 2, hub_mem(other % 2)),
                device_id_type=MESH,
            )

        for k in range(1, hubs):
            sum_copy(k, here).start()
        for k in range(1, hubs):
            sum_copy(k, (here + k) % hubs).wait_recv()
        total = jnp.sum(jnp.sum(sums[...], axis=0), keepdims=True)
        rows = float(groups * members * PER * BLK)
        result[...] = result[...] * (rows / total)[None]

        def back(k):
            other = (mem + k) % members
            return pltpu.make_async_remote_copy(
                src_ref=result.at[other],
                dst_ref=weights.at[role],
                send_sem=back_send.at[k],
                recv_sem=back_recv.at[role],
                device_id=(clu, other),
                device_id_type=MESH,
            )

        for k in range(1, members):
            back(k).start()
        weights[role] = result[mem]
        for c in range(HALF):
            share(role, c).wait_send()
            share(1 - role, c).wait_send()
        for k in range(1, hubs):
            sum_copy(k, here).wait_send()
        for k in range(1, members):
            back(k).wait_send()

    def returned(which):
        pltpu.make_async_remote_copy(
            src_ref=result.at[0],
            dst_ref=weights.at[which],
            send_sem=back_send.at[0],
            recv_sem=back_recv.at[which],
            device_id=(clu, hub_mem(which)),
            device_id_type=MESH,
        ).wait_recv()

    for which in (0, 1):
        @pl.when(mem != hub_mem(which))
        def _(which=which):
            returned(which)

    for block in range(PER):
        spot = 0
        for s in range(PER):
            spot = jnp.where(order_ref[0, mem * PER + s] == block, s, spot)
        out_ref[block : block + 1] = weights[spot // HALF, pl.ds(spot % HALF, 1)]


def solution(mesh):
    groups, members = mesh.shape["clu"], mesh.shape["mem"]

    def shards(embeddings, block_order):
        rows, width = embeddings.shape
        units = HALF * members // 2
        out = pl.pallas_call(
            functools.partial(kernel, groups, members),
            out_shape=jax.ShapeDtypeStruct((PER, BLK), jnp.float32),
            in_specs=[pl.BlockSpec(memory_space=pl.ANY)] * 2,
            out_specs=pl.BlockSpec(memory_space=pltpu.VMEM),
            scratch_shapes=[
                pltpu.SMEM(block_order.shape, jnp.int32),
                pltpu.VMEM((PER, BLK, width), jnp.bfloat16),
                pltpu.SemaphoreType.DMA((2,)),
                pltpu.VMEM((PER, BLK, width), jnp.bfloat16),
                pltpu.VMEM((units, UNIT, width), jnp.bfloat16),
                pltpu.VMEM((units, UNIT, BLK), jnp.float32),
                pltpu.VMEM((units, 2, 8, BLK), jnp.float32),
                pltpu.VMEM((units, UNIT, BLK), jnp.float32),
                pltpu.VMEM((members, 8, BLK), jnp.float32),
                pltpu.VMEM((2 * groups, 8, BLK), jnp.float32),
                pltpu.VMEM((2, 8, BLK), jnp.float32),
                pltpu.VMEM((units, UNIT), jnp.float32),
                pltpu.SemaphoreType.DMA((2, HALF)),
                pltpu.SemaphoreType.DMA((units, 2)),
                pltpu.SemaphoreType.DMA((units,)),
                pltpu.SemaphoreType.DMA((units,)),
                pltpu.SemaphoreType.DMA((2,)),
                pltpu.SemaphoreType.DMA((2 * groups,)),
                pltpu.SemaphoreType.DMA((2 * groups,)),
                pltpu.SemaphoreType.DMA((members,)),
                pltpu.SemaphoreType.DMA((2,)),
            ],
            compiler_params=pltpu.CompilerParams(
                collective_id=0, has_side_effects=True, vmem_limit_bytes=60 * 1024 * 1024
            ),
            cost_estimate=pl.CostEstimate(
                flops=2 * rows * rows * members * width // 6,
                bytes_accessed=rows * width * 2,
                transcendentals=rows * rows,
            ),
        )(block_order, embeddings.reshape(PER, BLK, width))
        return out.reshape(rows)

    return jax.shard_map(
        shards,
        mesh=mesh,
        in_specs=(P(("clu", "mem"), None), P("clu", None)),
        out_specs=P(("clu", "mem")),
        check_vma=False,
    )
```

```python
import functools

import jax
import jax.numpy as jnp
from jax import lax
from jax.experimental import pallas as pl
from jax.experimental.pallas import tpu as pltpu
from jax.sharding import PartitionSpec as P

BLK = 128
PER = 8
HALF = PER // 2
UNIT = 2 * BLK
MESH = pl.DeviceIdType.MESH


def kernel(
    groups, members, order_hbm, emb_hbm, out_ref,
    order_ref, emb_ref, load_sem, mine, buf, rowacc, colacc, across, hrow, result, sums, weights,
    partial, send_sem, recv_sem, pass_send, pass_recv, part_sem, sum_send, sum_recv, back_send, back_recv,
):
    chips = members // 2
    mid = chips // 2
    clu = lax.axis_index("clu")
    mem = lax.axis_index("mem")
    chip, core = mem // 2, mem % 2

    def hub_mem(which):
        return 2 * (mid - which)

    def mirrored(which, one_chip):
        return which * (chips - 1) + (1 - 2 * which) * one_chip

    def base_and_slot(which, seen, c):
        first = which * (c // 2) * c
        per_chip = HALF * (1 - which) + which * (2 - c // 2)
        cc = c - first
        near = per_chip + cc * mid + jnp.where(seen < mid, 0, seen - mid)
        far = per_chip + per_chip * mid + cc * (mid - 1) + seen
        place = jnp.where(seen == mid, cc, jnp.where(seen < mid - 1, far, near))
        return first * chips, first * chips + place

    hub_chip = jnp.logical_or(chip == mid, chip == mid - 1)
    is_hub = jnp.logical_and(hub_chip, core == 0)
    is_near = jnp.logical_and(hub_chip, core == 1)
    role = jnp.where(chip == mid - 1, 1, 0)
    hubs = 2 * groups
    everyone = groups * members
    events = HALF * chips
    near_events = HALF + HALF * mid

    load_order = pltpu.make_async_copy(order_hbm, order_ref, load_sem.at[0])
    load_emb = pltpu.make_async_copy(emb_hbm, emb_ref, load_sem.at[1])
    load_order.start()
    load_emb.start()
    barrier = pltpu.get_barrier_semaphore()

    @pl.when(is_hub)
    def _():
        def greet_all(k, _):
            flat = (clu * members + mem + k) % everyone
            pl.semaphore_signal(
                barrier, inc=1, device_id=(flat // members, flat % members),
                device_id_type=MESH,
            )
            return 0

        lax.fori_loop(1, everyone, greet_all, 0)

    @pl.when(jnp.logical_not(is_hub))
    def _():
        def greet_hub(g, _):
            for which in (0, 1):
                pl.semaphore_signal(
                    barrier, inc=1, device_id=(g, hub_mem(which)), device_id_type=MESH
                )
            return 0

        lax.fori_loop(0, groups, greet_hub, 0)

    @pl.when(is_near)
    def _():
        def greet(k, _):
            other = (mem + k) % members

            @pl.when(jnp.logical_and(other != hub_mem(0), other != hub_mem(1)))
            def _():
                pl.semaphore_signal(
                    barrier, inc=1, device_id=(clu, other), device_id_type=MESH
                )

            return 0

        lax.fori_loop(1, members, greet, 0)

    @pl.when(jnp.logical_not(hub_chip))
    def _():
        for which in (0, 1):
            pl.semaphore_signal(
                barrier, inc=1, device_id=(clu, hub_mem(which) + 1), device_id_type=MESH
            )

    load_order.wait()
    load_emb.wait()
    for s in range(PER):
        mine[s] = emb_ref[order_ref[0, mem * PER + s]]

    def share(which, c):
        seen = mirrored(which, chip)
        _, slot = base_and_slot(which, seen, c)
        return pltpu.make_async_remote_copy(
            src_ref=mine.at[which * HALF + c],
            dst_ref=buf.at[slot, pl.ds(pl.multiple_of(core * BLK, BLK), BLK)],
            send_sem=send_sem.at[which, c],
            recv_sem=recv_sem.at[slot, core],
            device_id=(clu, hub_mem(which) + jnp.where(seen < mid - 1, 0, 1)),
            device_id_type=MESH,
        )

    def at_event(e):
        i = e - HALF
        j = i - HALF * mid
        idx = i % mid
        near = jnp.where(idx == 0, mid - 1, mid + idx)
        seen = jnp.where(i < 0, mid, jnp.where(j < 0, near, j % (mid - 1)))
        c = jnp.where(i < 0, e, jnp.where(j < 0, i // mid, j // (mid - 1)))
        return base_and_slot(role, seen, c)

    def arrived(slot, half):
        pltpu.make_async_remote_copy(
            src_ref=mine.at[0],
            dst_ref=buf.at[slot, pl.ds(half * BLK, BLK)],
            send_sem=send_sem.at[0, 0],
            recv_sem=recv_sem.at[slot, half],
            device_id=(clu, hub_mem(0)),
            device_id_type=MESH,
        ).wait_recv()

    def passed(slot):
        return pltpu.make_async_remote_copy(
            src_ref=buf.at[slot],
            dst_ref=buf.at[slot],
            send_sem=pass_send.at[slot],
            recv_sem=pass_recv.at[slot],
            device_id=(clu, 2 * chip),
            device_id_type=MESH,
        )

    part_copy = pltpu.make_async_remote_copy(
        src_ref=partial,
        dst_ref=partial,
        send_sem=part_sem.at[0],
        recv_sem=part_sem.at[1],
        device_id=(clu, 2 * chip),
        device_id_type=MESH,
    )

    def norms(slot):
        wide = buf[slot].astype(jnp.float32)
        square = wide * wide
        part = square[:, :BLK]
        for k in range(1, square.shape[1] // BLK):
            part = part + square[:, k * BLK : (k + 1) * BLK]
        hrow[slot] = 0.5 * jnp.sum(part.T, axis=0, keepdims=True)
        colacc[slot] = jnp.zeros((2, 8, BLK), jnp.float32)
        return 0.5 * jnp.sum(part, axis=1, keepdims=True)

    def compare(base, slot, hcol):
        rowacc[...] = jnp.zeros_like(rowacc)
        left = jnp.broadcast_to(hcol, (UNIT, BLK))

        def tiles(q, count):
            for k in range(count):
                prod = lax.dot_general(
                    buf[slot], buf[q + k], (((1,), (1,)), ((), ())),
                    preferred_element_type=jnp.float32,
                )
                h = hrow[q + k]
                t0 = jnp.exp(prod[:, :BLK] - left - h[:, :BLK])
                t1 = jnp.exp(prod[:, BLK:] - left - h[:, BLK:])
                rowacc[...] += t0 + t1
                colacc[q + k, 0] += jnp.sum(t0.reshape(UNIT // 8, 8, BLK), axis=0)
                colacc[q + k, 1] += jnp.sum(t1.reshape(UNIT // 8, 8, BLK), axis=0)

        count = slot + 1 - base
        quads = count // 4

        def four(k, _):
            tiles(base + 4 * k, 4)
            return 0

        lax.fori_loop(0, quads, four, 0)

        @pl.when(count % 4 >= 2)
        def _():
            tiles(base + 4 * quads, 2)

        @pl.when(count % 2 == 1)
        def _():
            tiles(slot, 1)

        colacc[slot] = jnp.zeros((2, 8, BLK), jnp.float32)
        across[slot] = jnp.sum(rowacc[...].T, axis=0, keepdims=True)

    def density(slot):
        down = jnp.sum(colacc[slot], axis=1)
        return across[slot] + jnp.concatenate([down[:1], down[1:]], axis=1)

    @pl.when(jnp.logical_not(hub_chip))
    def _():
        pl.semaphore_wait(barrier, hubs + 2)
        first = jnp.where(chip < mid, 1, 0)

        def step(k, _):
            @pl.when(k < PER)
            def _():
                turn = k // HALF
                share(first * (1 - turn) + (1 - first) * turn, k % HALF).start()

            @pl.when(k >= HALF)
            def _():
                done = k - HALF
                turn = done // HALF
                share(first * (1 - turn) + (1 - first) * turn, done % HALF).wait_send()

            return 0

        lax.fori_loop(0, PER + HALF, step, 0)

    @pl.when(is_near)
    def _():
        pl.semaphore_wait(barrier, hubs + members - 3)
        for c in range(HALF):
            share(1 - role, c).start()
        for c in range(HALF):
            _, slot = base_and_slot(role, mid, c)
            buf[slot, BLK:] = mine[role * HALF + c]
        partial[...] = jnp.zeros_like(partial)

        def event(e, _):
            base, slot = at_event(e)
            arrived(slot, 0)

            @pl.when(e >= HALF)
            def _():
                arrived(slot, 1)

            passed(slot).start()
            compare(base, slot, norms(slot))
            return 0

        lax.fori_loop(0, near_events, event, 0)

        def fill(e, _):
            _, slot = at_event(e)
            partial[pl.ds(slot, 1)] = density(slot)
            return 0

        lax.fori_loop(0, near_events, fill, 0)
        part_copy.start()

        def drain(e, _):
            _, slot = at_event(e)
            passed(slot).wait_send()
            return 0

        lax.fori_loop(0, near_events, drain, 0)
        for c in range(HALF):
            share(1 - role, c).wait_send()
        part_copy.wait_send()

    @pl.when(is_hub)
    def _():
        pl.semaphore_wait(barrier, everyone - 1)
        for c in range(HALF):
            share(role, c).start()
        for c in range(HALF):
            share(1 - role, c).start()
        result[...] = jnp.zeros_like(result)

        def take(e, _):
            _, slot = at_event(e)
            passed(slot).wait_recv()
            norms(slot)
            across[slot] = jnp.zeros((1, UNIT), jnp.float32)
            return 0

        lax.fori_loop(0, near_events, take, 0)

        def event(e, _):
            base, slot = at_event(e)
            arrived(slot, 0)
            arrived(slot, 1)
            compare(base, slot, norms(slot))
            return 0

        lax.fori_loop(near_events, events, event, 0)
        part_copy.wait_recv()

        def finish(seen, _):
            holder = mirrored(role, seen)
            for c in range(HALF):
                _, slot = base_and_slot(role, seen, c)
                inverse = 1.0 / (density(slot) + partial[pl.ds(slot, 1)])
                for half in (0, 1):
                    result[2 * holder + half, c : c + 1] = inverse[
                        :, half * BLK : (half + 1) * BLK
                    ]
            return 0

        lax.fori_loop(0, chips, finish, 0)
        sums[2 * clu + role] = jnp.sum(result[...], axis=0)

        def back(k):
            other = (mem + k) % members
            return pltpu.make_async_remote_copy(
                src_ref=result.at[other],
                dst_ref=weights.at[role],
                send_sem=back_send.at[k],
                recv_sem=back_recv.at[role],
                device_id=(clu, other),
                device_id_type=MESH,
            )

        def sum_copy(k):
            flat = (clu * members + mem + k) % everyone
            return pltpu.make_async_remote_copy(
                src_ref=sums.at[2 * clu + role],
                dst_ref=sums.at[2 * clu + role],
                send_sem=sum_send.at[k],
                recv_sem=sum_recv.at[2 * clu + role],
                device_id=(flat // members, flat % members),
                device_id_type=MESH,
            )

        def tell(k, _):
            sum_copy(k).start()
            return 0

        def told(k, _):
            sum_copy(k).wait_send()
            return 0

        lax.fori_loop(1, everyone, tell, 0)
        for k in range(1, members):
            back(k).start()
        weights[role] = result[mem]
        for c in range(HALF):
            share(role, c).wait_send()
            share(1 - role, c).wait_send()
        lax.fori_loop(1, everyone, told, 0)
        for k in range(1, members):
            back(k).wait_send()

    def returned(which):
        pltpu.make_async_remote_copy(
            src_ref=result.at[0],
            dst_ref=weights.at[which],
            send_sem=back_send.at[0],
            recv_sem=back_recv.at[which],
            device_id=(clu, hub_mem(which)),
            device_id_type=MESH,
        ).wait_recv()

    for which in (0, 1):
        @pl.when(mem != hub_mem(which))
        def _(which=which):
            returned(which)

    for one in range(hubs):
        @pl.when(jnp.logical_or(clu != one // 2, mem != hub_mem(one % 2)))
        def _(one=one):
            pltpu.make_async_remote_copy(
                src_ref=sums.at[one],
                dst_ref=sums.at[one],
                send_sem=sum_send.at[0],
                recv_sem=sum_recv.at[one],
                device_id=(clu, hub_mem(0)),
                device_id_type=MESH,
            ).wait_recv()

    total = jnp.sum(jnp.sum(sums[...], axis=0), keepdims=True)
    scale = float(everyone * PER * BLK) / total
    for block in range(PER):
        spot = 0
        for s in range(PER):
            spot = jnp.where(order_ref[0, mem * PER + s] == block, s, spot)
        out_ref[block : block + 1] = weights[spot // HALF, pl.ds(spot % HALF, 1)] * scale


def solution(mesh):
    groups, members = mesh.shape["clu"], mesh.shape["mem"]

    def shards(embeddings, block_order):
        rows, width = embeddings.shape
        units = HALF * members // 2
        out = pl.pallas_call(
            functools.partial(kernel, groups, members),
            out_shape=jax.ShapeDtypeStruct((PER, BLK), jnp.float32),
            in_specs=[pl.BlockSpec(memory_space=pl.ANY)] * 2,
            out_specs=pl.BlockSpec(memory_space=pltpu.VMEM),
            scratch_shapes=[
                pltpu.SMEM(block_order.shape, jnp.int32),
                pltpu.VMEM((PER, BLK, width), jnp.bfloat16),
                pltpu.SemaphoreType.DMA((2,)),
                pltpu.VMEM((PER, BLK, width), jnp.bfloat16),
                pltpu.VMEM((units, UNIT, width), jnp.bfloat16),
                pltpu.VMEM((UNIT, BLK), jnp.float32),
                pltpu.VMEM((units, 2, 8, BLK), jnp.float32),
                pltpu.VMEM((units, 1, UNIT), jnp.float32),
                pltpu.VMEM((units, 1, UNIT), jnp.float32),
                pltpu.VMEM((members, 8, BLK), jnp.float32),
                pltpu.VMEM((2 * groups, 8, BLK), jnp.float32),
                pltpu.VMEM((2, 8, BLK), jnp.float32),
                pltpu.VMEM((units, UNIT), jnp.float32),
                pltpu.SemaphoreType.DMA((2, HALF)),
                pltpu.SemaphoreType.DMA((units, 2)),
                pltpu.SemaphoreType.DMA((units,)),
                pltpu.SemaphoreType.DMA((units,)),
                pltpu.SemaphoreType.DMA((2,)),
                pltpu.SemaphoreType.DMA((groups * members,)),
                pltpu.SemaphoreType.DMA((2 * groups,)),
                pltpu.SemaphoreType.DMA((members,)),
                pltpu.SemaphoreType.DMA((2,)),
            ],
            compiler_params=pltpu.CompilerParams(
                collective_id=0, has_side_effects=True, vmem_limit_bytes=60 * 1024 * 1024
            ),
            cost_estimate=pl.CostEstimate(
                flops=2 * rows * rows * members * width // 6,
                bytes_accessed=rows * width * 2,
                transcendentals=rows * rows,
            ),
        )(block_order, embeddings.reshape(PER, BLK, width))
        return out.reshape(rows)

    return jax.shard_map(
        shards,
        mesh=mesh,
        in_specs=(P(("clu", "mem"), None), P("clu", None)),
        out_specs=P(("clu", "mem")),
        check_vma=False,
    )
```

```python
import functools

import jax
import jax.numpy as jnp
from jax import lax
from jax.experimental import pallas as pl
from jax.experimental.pallas import tpu as pltpu
from jax.sharding import PartitionSpec as P

BLK = 128
PER = 8
HALF = PER // 2
UNIT = 2 * BLK
MESH = pl.DeviceIdType.MESH


def kernel(
    groups, members, order_hbm, emb_hbm, out_ref,
    order_ref, emb_ref, load_sem, mine, buf, turned, rowacc, colacc, across, hrow, result, sums, weights,
    partial, send_sem, recv_sem, pass_send, pass_recv, part_sem, sum_send, sum_recv, back_send, back_recv,
):
    chips = members // 2
    mid = chips // 2
    clu = lax.axis_index("clu")
    mem = lax.axis_index("mem")
    chip, core = mem // 2, mem % 2

    def hub_mem(which):
        return 2 * (mid - which)

    def mirrored(which, one_chip):
        return which * (chips - 1) + (1 - 2 * which) * one_chip

    def base_and_slot(which, seen, c):
        first = which * (c // 2) * c
        per_chip = HALF * (1 - which) + which * (2 - c // 2)
        cc = c - first
        near = per_chip + cc * mid + jnp.where(seen < mid, 0, seen - mid)
        far = per_chip + per_chip * mid + cc * (mid - 1) + seen
        place = jnp.where(seen == mid, cc, jnp.where(seen < mid - 1, far, near))
        return first * chips, first * chips + place

    hub_chip = jnp.logical_or(chip == mid, chip == mid - 1)
    is_hub = jnp.logical_and(hub_chip, core == 0)
    is_near = jnp.logical_and(hub_chip, core == 1)
    role = jnp.where(chip == mid - 1, 1, 0)
    hubs = 2 * groups
    everyone = groups * members
    events = HALF * chips
    near_events = HALF + HALF * mid

    load_order = pltpu.make_async_copy(order_hbm, order_ref, load_sem.at[0])
    load_emb = pltpu.make_async_copy(emb_hbm, emb_ref, load_sem.at[1])
    load_order.start()
    load_emb.start()
    barrier = pltpu.get_barrier_semaphore()

    @pl.when(is_hub)
    def _():
        def greet_all(k, _):
            flat = (clu * members + mem + k) % everyone
            pl.semaphore_signal(
                barrier, inc=1, device_id=(flat // members, flat % members),
                device_id_type=MESH,
            )
            return 0

        lax.fori_loop(1, everyone, greet_all, 0)

    @pl.when(jnp.logical_not(is_hub))
    def _():
        def greet_hub(g, _):
            for which in (0, 1):
                pl.semaphore_signal(
                    barrier, inc=1, device_id=(g, hub_mem(which)), device_id_type=MESH
                )
            return 0

        lax.fori_loop(0, groups, greet_hub, 0)

    @pl.when(is_near)
    def _():
        def greet(k, _):
            other = (mem + k) % members

            @pl.when(jnp.logical_and(other != hub_mem(0), other != hub_mem(1)))
            def _():
                pl.semaphore_signal(
                    barrier, inc=1, device_id=(clu, other), device_id_type=MESH
                )

            return 0

        lax.fori_loop(1, members, greet, 0)

    @pl.when(jnp.logical_not(hub_chip))
    def _():
        for which in (0, 1):
            pl.semaphore_signal(
                barrier, inc=1, device_id=(clu, hub_mem(which) + 1), device_id_type=MESH
            )

    load_order.wait()
    load_emb.wait()
    for s in range(PER):
        mine[s] = emb_ref[order_ref[0, mem * PER + s]]

    def share(which, c):
        seen = mirrored(which, chip)
        _, slot = base_and_slot(which, seen, c)
        return pltpu.make_async_remote_copy(
            src_ref=mine.at[which * HALF + c],
            dst_ref=buf.at[slot, pl.ds(pl.multiple_of(core * BLK, BLK), BLK)],
            send_sem=send_sem.at[which, c],
            recv_sem=recv_sem.at[slot, core],
            device_id=(clu, hub_mem(which) + jnp.where(seen < mid - 1, 0, 1)),
            device_id_type=MESH,
        )

    def at_event(e):
        i = e - HALF
        j = i - HALF * mid
        idx = i % mid
        near = jnp.where(idx == 0, mid - 1, mid + idx)
        seen = jnp.where(i < 0, mid, jnp.where(j < 0, near, j % (mid - 1)))
        c = jnp.where(i < 0, e, jnp.where(j < 0, i // mid, j // (mid - 1)))
        return base_and_slot(role, seen, c)

    def arrived(slot, half):
        pltpu.make_async_remote_copy(
            src_ref=mine.at[0],
            dst_ref=buf.at[slot, pl.ds(half * BLK, BLK)],
            send_sem=send_sem.at[0, 0],
            recv_sem=recv_sem.at[slot, half],
            device_id=(clu, hub_mem(0)),
            device_id_type=MESH,
        ).wait_recv()

    def passed(slot):
        return pltpu.make_async_remote_copy(
            src_ref=buf.at[slot],
            dst_ref=buf.at[slot],
            send_sem=pass_send.at[slot],
            recv_sem=pass_recv.at[slot],
            device_id=(clu, 2 * chip),
            device_id_type=MESH,
        )

    part_copy = pltpu.make_async_remote_copy(
        src_ref=partial,
        dst_ref=partial,
        send_sem=part_sem.at[0],
        recv_sem=part_sem.at[1],
        device_id=(clu, 2 * chip),
        device_id_type=MESH,
    )

    def norms(slot):
        wide = buf[slot].astype(jnp.float32)
        turned[slot] = wide.T.astype(jnp.bfloat16)
        square = wide * wide
        part = square[:, :BLK]
        for k in range(1, square.shape[1] // BLK):
            part = part + square[:, k * BLK : (k + 1) * BLK]
        hrow[slot] = 0.5 * jnp.sum(part.T, axis=0, keepdims=True)
        colacc[slot] = jnp.zeros((2, 8, BLK), jnp.float32)
        return 0.5 * jnp.sum(part, axis=1, keepdims=True)

    def compare(base, slot, hcol):
        rowacc[...] = jnp.zeros_like(rowacc)
        left = jnp.broadcast_to(hcol, (UNIT, BLK))

        def tiles(q, count):
            for k in range(count):
                prod = lax.dot_general(
                    buf[slot], turned[q + k], (((1,), (0,)), ((), ())),
                    preferred_element_type=jnp.float32,
                )
                h = hrow[q + k]
                t0 = jnp.exp(prod[:, :BLK] - left - h[:, :BLK])
                t1 = jnp.exp(prod[:, BLK:] - left - h[:, BLK:])
                rowacc[...] += t0 + t1
                colacc[q + k, 0] += jnp.sum(t0.reshape(UNIT // 8, 8, BLK), axis=0)
                colacc[q + k, 1] += jnp.sum(t1.reshape(UNIT // 8, 8, BLK), axis=0)

        count = slot + 1 - base
        quads = count // 4

        def four(k, _):
            tiles(base + 4 * k, 4)
            return 0

        lax.fori_loop(0, quads, four, 0)

        @pl.when(count % 4 >= 2)
        def _():
            tiles(base + 4 * quads, 2)

        @pl.when(count % 2 == 1)
        def _():
            tiles(slot, 1)

        colacc[slot] = jnp.zeros((2, 8, BLK), jnp.float32)
        across[slot] = jnp.sum(rowacc[...].T, axis=0, keepdims=True)

    def density(slot):
        down = jnp.sum(colacc[slot], axis=1)
        return across[slot] + jnp.concatenate([down[:1], down[1:]], axis=1)

    @pl.when(jnp.logical_not(hub_chip))
    def _():
        pl.semaphore_wait(barrier, hubs + 2)
        first = jnp.where(chip < mid, 1, 0)

        def step(k, _):
            @pl.when(k < PER)
            def _():
                turn = k // HALF
                share(first * (1 - turn) + (1 - first) * turn, k % HALF).start()

            @pl.when(k >= HALF)
            def _():
                done = k - HALF
                turn = done // HALF
                share(first * (1 - turn) + (1 - first) * turn, done % HALF).wait_send()

            return 0

        lax.fori_loop(0, PER + HALF, step, 0)

    @pl.when(is_near)
    def _():
        pl.semaphore_wait(barrier, hubs + members - 3)
        for c in range(HALF):
            share(1 - role, c).start()
        for c in range(HALF):
            _, slot = base_and_slot(role, mid, c)
            buf[slot, BLK:] = mine[role * HALF + c]
        partial[...] = jnp.zeros_like(partial)

        def event(e, _):
            base, slot = at_event(e)
            arrived(slot, 0)

            @pl.when(e >= HALF)
            def _():
                arrived(slot, 1)

            passed(slot).start()
            compare(base, slot, norms(slot))
            return 0

        lax.fori_loop(0, near_events, event, 0)

        def fill(e, _):
            _, slot = at_event(e)
            partial[pl.ds(slot, 1)] = density(slot)
            return 0

        lax.fori_loop(0, near_events, fill, 0)
        part_copy.start()

        def drain(e, _):
            _, slot = at_event(e)
            passed(slot).wait_send()
            return 0

        lax.fori_loop(0, near_events, drain, 0)
        for c in range(HALF):
            share(1 - role, c).wait_send()
        part_copy.wait_send()

    @pl.when(is_hub)
    def _():
        pl.semaphore_wait(barrier, everyone - 1)
        for c in range(HALF):
            share(role, c).start()
        for c in range(HALF):
            share(1 - role, c).start()
        result[...] = jnp.zeros_like(result)

        def take(e, _):
            _, slot = at_event(e)
            passed(slot).wait_recv()
            norms(slot)
            across[slot] = jnp.zeros((1, UNIT), jnp.float32)
            return 0

        lax.fori_loop(0, near_events, take, 0)

        def event(e, _):
            base, slot = at_event(e)
            arrived(slot, 0)
            arrived(slot, 1)
            compare(base, slot, norms(slot))
            return 0

        lax.fori_loop(near_events, events, event, 0)
        part_copy.wait_recv()

        def finish(seen, _):
            holder = mirrored(role, seen)
            for c in range(HALF):
                _, slot = base_and_slot(role, seen, c)
                inverse = 1.0 / (density(slot) + partial[pl.ds(slot, 1)])
                for half in (0, 1):
                    result[2 * holder + half, c : c + 1] = inverse[
                        :, half * BLK : (half + 1) * BLK
                    ]
            return 0

        lax.fori_loop(0, chips, finish, 0)
        sums[2 * clu + role] = jnp.sum(result[...], axis=0)

        def back(k):
            other = (mem + k) % members
            return pltpu.make_async_remote_copy(
                src_ref=result.at[other],
                dst_ref=weights.at[role],
                send_sem=back_send.at[k],
                recv_sem=back_recv.at[role],
                device_id=(clu, other),
                device_id_type=MESH,
            )

        def sum_copy(k):
            flat = (clu * members + mem + k) % everyone
            return pltpu.make_async_remote_copy(
                src_ref=sums.at[2 * clu + role],
                dst_ref=sums.at[2 * clu + role],
                send_sem=sum_send.at[k],
                recv_sem=sum_recv.at[2 * clu + role],
                device_id=(flat // members, flat % members),
                device_id_type=MESH,
            )

        def tell(k, _):
            sum_copy(k).start()
            return 0

        def told(k, _):
            sum_copy(k).wait_send()
            return 0

        lax.fori_loop(1, everyone, tell, 0)
        for k in range(1, members):
            back(k).start()
        weights[role] = result[mem]
        for c in range(HALF):
            share(role, c).wait_send()
            share(1 - role, c).wait_send()
        lax.fori_loop(1, everyone, told, 0)
        for k in range(1, members):
            back(k).wait_send()

    def returned(which):
        pltpu.make_async_remote_copy(
            src_ref=result.at[0],
            dst_ref=weights.at[which],
            send_sem=back_send.at[0],
            recv_sem=back_recv.at[which],
            device_id=(clu, hub_mem(which)),
            device_id_type=MESH,
        ).wait_recv()

    for which in (0, 1):
        @pl.when(mem != hub_mem(which))
        def _(which=which):
            returned(which)

    for one in range(hubs):
        @pl.when(jnp.logical_or(clu != one // 2, mem != hub_mem(one % 2)))
        def _(one=one):
            pltpu.make_async_remote_copy(
                src_ref=sums.at[one],
                dst_ref=sums.at[one],
                send_sem=sum_send.at[0],
                recv_sem=sum_recv.at[one],
                device_id=(clu, hub_mem(0)),
                device_id_type=MESH,
            ).wait_recv()

    total = jnp.sum(jnp.sum(sums[...], axis=0), keepdims=True)
    scale = float(everyone * PER * BLK) / total
    for block in range(PER):
        spot = 0
        for s in range(PER):
            spot = jnp.where(order_ref[0, mem * PER + s] == block, s, spot)
        out_ref[block : block + 1] = weights[spot // HALF, pl.ds(spot % HALF, 1)] * scale


def solution(mesh):
    groups, members = mesh.shape["clu"], mesh.shape["mem"]

    def shards(embeddings, block_order):
        rows, width = embeddings.shape
        units = HALF * members // 2
        out = pl.pallas_call(
            functools.partial(kernel, groups, members),
            out_shape=jax.ShapeDtypeStruct((PER, BLK), jnp.float32),
            in_specs=[pl.BlockSpec(memory_space=pl.ANY)] * 2,
            out_specs=pl.BlockSpec(memory_space=pltpu.VMEM),
            scratch_shapes=[
                pltpu.SMEM(block_order.shape, jnp.int32),
                pltpu.VMEM((PER, BLK, width), jnp.bfloat16),
                pltpu.SemaphoreType.DMA((2,)),
                pltpu.VMEM((PER, BLK, width), jnp.bfloat16),
                pltpu.VMEM((units, UNIT, width), jnp.bfloat16),
                pltpu.VMEM((units, width, UNIT), jnp.bfloat16),
                pltpu.VMEM((UNIT, BLK), jnp.float32),
                pltpu.VMEM((units, 2, 8, BLK), jnp.float32),
                pltpu.VMEM((units, 1, UNIT), jnp.float32),
                pltpu.VMEM((units, 1, UNIT), jnp.float32),
                pltpu.VMEM((members, 8, BLK), jnp.float32),
                pltpu.VMEM((2 * groups, 8, BLK), jnp.float32),
                pltpu.VMEM((2, 8, BLK), jnp.float32),
                pltpu.VMEM((units, UNIT), jnp.float32),
                pltpu.SemaphoreType.DMA((2, HALF)),
                pltpu.SemaphoreType.DMA((units, 2)),
                pltpu.SemaphoreType.DMA((units,)),
                pltpu.SemaphoreType.DMA((units,)),
                pltpu.SemaphoreType.DMA((2,)),
                pltpu.SemaphoreType.DMA((groups * members,)),
                pltpu.SemaphoreType.DMA((2 * groups,)),
                pltpu.SemaphoreType.DMA((members,)),
                pltpu.SemaphoreType.DMA((2,)),
            ],
            compiler_params=pltpu.CompilerParams(
                collective_id=0, has_side_effects=True, vmem_limit_bytes=58 * 1024 * 1024
            ),
            cost_estimate=pl.CostEstimate(
                flops=2 * rows * rows * members * width // 6,
                bytes_accessed=rows * width * 2,
                transcendentals=rows * rows,
            ),
        )(block_order, embeddings.reshape(PER, BLK, width))
        return out.reshape(rows)

    return jax.shard_map(
        shards,
        mesh=mesh,
        in_specs=(P(("clu", "mem"), None), P("clu", None)),
        out_specs=P(("clu", "mem")),
        check_vma=False,
    )
```

```python
import functools

import jax
import jax.numpy as jnp
from jax import lax
from jax.experimental import pallas as pl
from jax.experimental.pallas import tpu as pltpu
from jax.sharding import PartitionSpec as P

BLK = 128
PER = 8
HALF = PER // 2
UNIT = 2 * BLK
MESH = pl.DeviceIdType.MESH


def kernel(
    groups, members, order_hbm, emb_hbm, out_ref,
    order_ref, emb_ref, load_sem, mine, buf, turned, rowacc, colacc, across, hrow, result, sums, weights,
    partial, send_sem, recv_sem, pass_send, pass_recv, part_sem, sum_send, sum_recv, back_send, back_recv,
):
    chips = members // 2
    mid = chips // 2
    clu = lax.axis_index("clu")
    mem = lax.axis_index("mem")
    chip, core = mem // 2, mem % 2

    def hub_mem(which):
        return 2 * (mid - which)

    def mirrored(which, one_chip):
        return which * (chips - 1) + (1 - 2 * which) * one_chip

    def base_and_slot(which, seen, c):
        first = which * (c // 2) * c
        per_chip = HALF * (1 - which) + which * (2 - c // 2)
        cc = c - first
        near = per_chip + cc * mid + jnp.where(seen < mid, 0, seen - mid)
        far = per_chip + per_chip * mid + cc * (mid - 1) + seen
        place = jnp.where(seen == mid, cc, jnp.where(seen < mid - 1, far, near))
        return first * chips, first * chips + place

    hub_chip = jnp.logical_or(chip == mid, chip == mid - 1)
    is_hub = jnp.logical_and(hub_chip, core == 0)
    is_near = jnp.logical_and(hub_chip, core == 1)
    role = jnp.where(chip == mid - 1, 1, 0)
    hubs = 2 * groups
    everyone = groups * members
    events = HALF * chips
    near_events = HALF + HALF * mid

    load_order = pltpu.make_async_copy(order_hbm, order_ref, load_sem.at[0])
    load_emb = pltpu.make_async_copy(emb_hbm, emb_ref, load_sem.at[1])
    load_order.start()
    load_emb.start()
    barrier = pltpu.get_barrier_semaphore()

    @pl.when(is_hub)
    def _():
        def greet_all(k, _):
            flat = (clu * members + mem + k) % everyone
            pl.semaphore_signal(
                barrier, inc=1, device_id=(flat // members, flat % members),
                device_id_type=MESH,
            )
            return 0

        lax.fori_loop(1, everyone, greet_all, 0)

    @pl.when(jnp.logical_not(is_hub))
    def _():
        def greet_hub(g, _):
            for which in (0, 1):
                pl.semaphore_signal(
                    barrier, inc=1, device_id=(g, hub_mem(which)), device_id_type=MESH
                )
            return 0

        lax.fori_loop(0, groups, greet_hub, 0)

    @pl.when(is_near)
    def _():
        def greet(k, _):
            other = (mem + k) % members

            @pl.when(jnp.logical_and(other != hub_mem(0), other != hub_mem(1)))
            def _():
                pl.semaphore_signal(
                    barrier, inc=1, device_id=(clu, other), device_id_type=MESH
                )

            return 0

        lax.fori_loop(1, members, greet, 0)

    @pl.when(jnp.logical_not(hub_chip))
    def _():
        for which in (0, 1):
            pl.semaphore_signal(
                barrier, inc=1, device_id=(clu, hub_mem(which) + 1), device_id_type=MESH
            )

    load_order.wait()
    load_emb.wait()

    def fetch(s):
        return emb_ref[order_ref[0, mem * PER + s]]

    def share(which, c):
        seen = mirrored(which, chip)
        _, slot = base_and_slot(which, seen, c)
        return pltpu.make_async_remote_copy(
            src_ref=mine.at[which * HALF + c],
            dst_ref=buf.at[slot, pl.ds(pl.multiple_of(core * BLK, BLK), BLK)],
            send_sem=send_sem.at[which, c],
            recv_sem=recv_sem.at[slot, core],
            device_id=(clu, hub_mem(which) + jnp.where(seen < mid - 1, 0, 1)),
            device_id_type=MESH,
        )

    def at_event(e):
        i = e - HALF
        j = i - HALF * mid
        idx = i % mid
        near = jnp.where(idx == 0, mid - 1, mid + idx)
        seen = jnp.where(i < 0, mid, jnp.where(j < 0, near, j % (mid - 1)))
        c = jnp.where(i < 0, e, jnp.where(j < 0, i // mid, j // (mid - 1)))
        return base_and_slot(role, seen, c)

    def arrived(slot, half):
        pltpu.make_async_remote_copy(
            src_ref=mine.at[0],
            dst_ref=buf.at[slot, pl.ds(half * BLK, BLK)],
            send_sem=send_sem.at[0, 0],
            recv_sem=recv_sem.at[slot, half],
            device_id=(clu, hub_mem(0)),
            device_id_type=MESH,
        ).wait_recv()

    def passed(slot):
        return pltpu.make_async_remote_copy(
            src_ref=buf.at[slot],
            dst_ref=buf.at[slot],
            send_sem=pass_send.at[slot],
            recv_sem=pass_recv.at[slot],
            device_id=(clu, 2 * chip),
            device_id_type=MESH,
        )

    part_copy = pltpu.make_async_remote_copy(
        src_ref=partial,
        dst_ref=partial,
        send_sem=part_sem.at[0],
        recv_sem=part_sem.at[1],
        device_id=(clu, 2 * chip),
        device_id_type=MESH,
    )

    def norms(slot):
        wide = buf[slot].astype(jnp.float32)
        turned[slot] = wide.T.astype(jnp.bfloat16)
        square = wide * wide
        part = square[:, :BLK]
        for k in range(1, square.shape[1] // BLK):
            part = part + square[:, k * BLK : (k + 1) * BLK]
        hrow[slot] = 0.5 * jnp.sum(part.T, axis=0, keepdims=True)
        colacc[slot] = jnp.zeros((2, 8, BLK), jnp.float32)
        return 0.5 * jnp.sum(part, axis=1, keepdims=True)

    def compare(base, slot, hcol):
        rowacc[...] = jnp.zeros_like(rowacc)
        left = jnp.broadcast_to(hcol, (UNIT, BLK))

        def tiles(q, count):
            for k in range(count):
                prod = lax.dot_general(
                    buf[slot], turned[q + k], (((1,), (0,)), ((), ())),
                    preferred_element_type=jnp.float32,
                )
                h = hrow[q + k]
                t0 = jnp.exp(prod[:, :BLK] - left - h[:, :BLK])
                t1 = jnp.exp(prod[:, BLK:] - left - h[:, BLK:])
                rowacc[...] += t0 + t1
                colacc[q + k, 0] += jnp.sum(t0.reshape(UNIT // 8, 8, BLK), axis=0)
                colacc[q + k, 1] += jnp.sum(t1.reshape(UNIT // 8, 8, BLK), axis=0)

        count = slot + 1 - base
        quads = count // 4

        def four(k, _):
            tiles(base + 4 * k, 4)
            return 0

        lax.fori_loop(0, quads, four, 0)

        @pl.when(count % 4 >= 2)
        def _():
            tiles(base + 4 * quads, 2)

        @pl.when(count % 2 == 1)
        def _():
            tiles(slot, 1)

        colacc[slot] = jnp.zeros((2, 8, BLK), jnp.float32)
        across[slot] = jnp.sum(rowacc[...].T, axis=0, keepdims=True)

    def density(slot):
        down = jnp.sum(colacc[slot], axis=1)
        return across[slot] + jnp.concatenate([down[:1], down[1:]], axis=1)

    @pl.when(jnp.logical_not(hub_chip))
    def _():
        pl.semaphore_wait(barrier, hubs + 2)
        first = jnp.where(chip < mid, 1, 0)

        def step(k, _):
            @pl.when(k < PER)
            def _():
                turn = k // HALF
                which = first * (1 - turn) + (1 - first) * turn
                mine[which * HALF + k % HALF] = fetch(which * HALF + k % HALF)
                share(which, k % HALF).start()

            @pl.when(k >= HALF)
            def _():
                done = k - HALF
                turn = done // HALF
                share(first * (1 - turn) + (1 - first) * turn, done % HALF).wait_send()

            return 0

        lax.fori_loop(0, PER + HALF, step, 0)

    @pl.when(is_near)
    def _():
        pl.semaphore_wait(barrier, hubs + members - 3)
        for c in range(HALF):
            mine[(1 - role) * HALF + c] = fetch((1 - role) * HALF + c)
            share(1 - role, c).start()
        for c in range(HALF):
            _, slot = base_and_slot(role, mid, c)
            buf[slot, BLK:] = fetch(role * HALF + c)
        partial[...] = jnp.zeros_like(partial)

        def event(e, _):
            base, slot = at_event(e)
            arrived(slot, 0)

            @pl.when(e >= HALF)
            def _():
                arrived(slot, 1)

            passed(slot).start()
            compare(base, slot, norms(slot))
            return 0

        lax.fori_loop(0, near_events, event, 0)

        def fill(e, _):
            _, slot = at_event(e)
            partial[pl.ds(slot, 1)] = density(slot)
            return 0

        lax.fori_loop(0, near_events, fill, 0)
        part_copy.start()

        def drain(e, _):
            _, slot = at_event(e)
            passed(slot).wait_send()
            return 0

        lax.fori_loop(0, near_events, drain, 0)
        for c in range(HALF):
            share(1 - role, c).wait_send()
        part_copy.wait_send()

    @pl.when(is_hub)
    def _():
        pl.semaphore_wait(barrier, everyone - 1)
        for which in (1 - role, role):
            for c in range(HALF):
                mine[which * HALF + c] = fetch(which * HALF + c)
                share(which, c).start()
        result[...] = jnp.zeros_like(result)

        def take(e, _):
            _, slot = at_event(e)
            passed(slot).wait_recv()
            norms(slot)
            across[slot] = jnp.zeros((1, UNIT), jnp.float32)
            return 0

        lax.fori_loop(0, near_events, take, 0)

        def event(e, _):
            base, slot = at_event(e)
            arrived(slot, 0)
            arrived(slot, 1)
            compare(base, slot, norms(slot))
            return 0

        lax.fori_loop(near_events, events, event, 0)
        part_copy.wait_recv()

        def finish(seen, _):
            holder = mirrored(role, seen)
            for c in range(HALF):
                _, slot = base_and_slot(role, seen, c)
                inverse = 1.0 / (density(slot) + partial[pl.ds(slot, 1)])
                for half in (0, 1):
                    result[2 * holder + half, c : c + 1] = inverse[
                        :, half * BLK : (half + 1) * BLK
                    ]
            return 0

        lax.fori_loop(0, chips, finish, 0)
        own = jnp.sum(jnp.sum(result[...], axis=0), axis=0, keepdims=True)
        result[:, HALF : HALF + 1] = jnp.broadcast_to(own[None], (members, 1, BLK))

        def back(k):
            other = (mem + k) % members
            return pltpu.make_async_remote_copy(
                src_ref=result.at[other],
                dst_ref=weights.at[role],
                send_sem=back_send.at[k],
                recv_sem=back_recv.at[role],
                device_id=(clu, other),
                device_id_type=MESH,
            )

        def sum_copy(k):
            flat = (clu * members + k) % everyone
            return pltpu.make_async_remote_copy(
                src_ref=result.at[mem],
                dst_ref=sums.at[2 * clu + role],
                send_sem=sum_send.at[k],
                recv_sem=sum_recv.at[2 * clu + role],
                device_id=(flat // members, flat % members),
                device_id_type=MESH,
            )

        def tell(k, _):
            sum_copy(k).start()
            return 0

        def told(k, _):
            sum_copy(k).wait_send()
            return 0

        lax.fori_loop(members, everyone, tell, 0)
        for k in range(1, members):
            back(k).start()
        weights[role] = result[mem]
        for c in range(HALF):
            share(role, c).wait_send()
            share(1 - role, c).wait_send()
        lax.fori_loop(members, everyone, told, 0)
        for k in range(1, members):
            back(k).wait_send()

    def returned(which):
        pltpu.make_async_remote_copy(
            src_ref=result.at[0],
            dst_ref=weights.at[which],
            send_sem=back_send.at[0],
            recv_sem=back_recv.at[which],
            device_id=(clu, hub_mem(which)),
            device_id_type=MESH,
        ).wait_recv()

    for which in (0, 1):
        @pl.when(mem != hub_mem(which))
        def _(which=which):
            returned(which)

    for one in range(hubs):
        @pl.when(clu == one // 2)
        def _(one=one):
            sums[one] = weights[one % 2]

        @pl.when(clu != one // 2)
        def _(one=one):
            pltpu.make_async_remote_copy(
                src_ref=sums.at[one],
                dst_ref=sums.at[one],
                send_sem=sum_send.at[0],
                recv_sem=sum_recv.at[one],
                device_id=(clu, hub_mem(0)),
                device_id_type=MESH,
            ).wait_recv()

    total = jnp.sum(jnp.sum(sums[...], axis=0)[HALF : HALF + 1], keepdims=True)
    scale = float(everyone * PER * BLK) / total
    for block in range(PER):
        spot = 0
        for s in range(PER):
            spot = jnp.where(order_ref[0, mem * PER + s] == block, s, spot)
        out_ref[block : block + 1] = weights[spot // HALF, pl.ds(spot % HALF, 1)] * scale


def solution(mesh):
    groups, members = mesh.shape["clu"], mesh.shape["mem"]

    def shards(embeddings, block_order):
        rows, width = embeddings.shape
        units = HALF * members // 2
        out = pl.pallas_call(
            functools.partial(kernel, groups, members),
            out_shape=jax.ShapeDtypeStruct((PER, BLK), jnp.float32),
            in_specs=[pl.BlockSpec(memory_space=pl.ANY)] * 2,
            out_specs=pl.BlockSpec(memory_space=pltpu.VMEM),
            scratch_shapes=[
                pltpu.SMEM(block_order.shape, jnp.int32),
                pltpu.VMEM((PER, BLK, width), jnp.bfloat16),
                pltpu.SemaphoreType.DMA((2,)),
                pltpu.VMEM((PER, BLK, width), jnp.bfloat16),
                pltpu.VMEM((units, UNIT, width), jnp.bfloat16),
                pltpu.VMEM((units, width, UNIT), jnp.bfloat16),
                pltpu.VMEM((UNIT, BLK), jnp.float32),
                pltpu.VMEM((units, 2, 8, BLK), jnp.float32),
                pltpu.VMEM((units, 1, UNIT), jnp.float32),
                pltpu.VMEM((units, 1, UNIT), jnp.float32),
                pltpu.VMEM((members, 8, BLK), jnp.float32),
                pltpu.VMEM((2 * groups, 8, BLK), jnp.float32),
                pltpu.VMEM((2, 8, BLK), jnp.float32),
                pltpu.VMEM((units, UNIT), jnp.float32),
                pltpu.SemaphoreType.DMA((2, HALF)),
                pltpu.SemaphoreType.DMA((units, 2)),
                pltpu.SemaphoreType.DMA((units,)),
                pltpu.SemaphoreType.DMA((units,)),
                pltpu.SemaphoreType.DMA((2,)),
                pltpu.SemaphoreType.DMA((groups * members,)),
                pltpu.SemaphoreType.DMA((2 * groups,)),
                pltpu.SemaphoreType.DMA((members,)),
                pltpu.SemaphoreType.DMA((2,)),
            ],
            compiler_params=pltpu.CompilerParams(
                collective_id=0, has_side_effects=True, vmem_limit_bytes=58 * 1024 * 1024
            ),
            cost_estimate=pl.CostEstimate(
                flops=2 * rows * rows * members * width // 6,
                bytes_accessed=rows * width * 2,
                transcendentals=rows * rows,
            ),
        )(block_order, embeddings.reshape(PER, BLK, width))
        return out.reshape(rows)

    return jax.shard_map(
        shards,
        mesh=mesh,
        in_specs=(P(("clu", "mem"), None), P("clu", None)),
        out_specs=P(("clu", "mem")),
        check_vma=False,
    )
```

```python
import functools

import jax
import jax.numpy as jnp
from jax import lax
from jax.experimental import pallas as pl
from jax.experimental.pallas import tpu as pltpu
from jax.sharding import PartitionSpec as P

BLK = 128
PER = 8
HALF = PER // 2
UNIT = 2 * BLK
MESH = pl.DeviceIdType.MESH


def kernel(
    groups, members, order_hbm, emb_hbm, out_ref,
    order_ref, emb_ref, load_sem, mine, buf, turned, rowacc, colacc, across, hrow, result, sums, weights,
    partial, send_sem, recv_sem, pass_send, pass_recv, part_sem, sum_send, sum_recv, back_send, back_recv,
):
    chips = members // 2
    mid = chips // 2
    clu = lax.axis_index("clu")
    mem = lax.axis_index("mem")
    chip, core = mem // 2, mem % 2

    def hub_mem(which):
        return 2 * (mid - which)

    def mirrored(which, one_chip):
        return which * (chips - 1) + (1 - 2 * which) * one_chip

    def base_and_slot(which, seen, c):
        first = which * (c // 2) * c
        per_chip = HALF * (1 - which) + which * (2 - c // 2)
        cc = c - first
        near = per_chip + cc * mid + jnp.where(seen < mid, 0, seen - mid)
        far = per_chip + per_chip * mid + cc * (mid - 1) + seen
        place = jnp.where(seen == mid, cc, jnp.where(seen < mid - 1, far, near))
        return first * chips, first * chips + place

    hub_chip = jnp.logical_or(chip == mid, chip == mid - 1)
    is_hub = jnp.logical_and(hub_chip, core == 0)
    is_near = jnp.logical_and(hub_chip, core == 1)
    role = jnp.where(chip == mid - 1, 1, 0)
    hubs = 2 * groups
    everyone = groups * members
    events = HALF * chips
    near_events = HALF + HALF * mid

    load_order = pltpu.make_async_copy(order_hbm, order_ref, load_sem.at[0])
    load_emb = pltpu.make_async_copy(emb_hbm, emb_ref, load_sem.at[1])
    load_order.start()
    load_emb.start()
    barrier = pltpu.get_barrier_semaphore()

    @pl.when(is_hub)
    def _():
        def greet_all(k, _):
            flat = (clu * members + mem + k) % everyone
            pl.semaphore_signal(
                barrier, inc=1, device_id=(flat // members, flat % members),
                device_id_type=MESH,
            )
            return 0

        lax.fori_loop(1, everyone, greet_all, 0)

    @pl.when(jnp.logical_not(is_hub))
    def _():
        def greet_hub(g, _):
            for which in (0, 1):
                pl.semaphore_signal(
                    barrier, inc=1, device_id=(g, hub_mem(which)), device_id_type=MESH
                )
            return 0

        lax.fori_loop(0, groups, greet_hub, 0)

    @pl.when(is_near)
    def _():
        def greet(k, _):
            other = (mem + k) % members

            @pl.when(jnp.logical_and(other != hub_mem(0), other != hub_mem(1)))
            def _():
                pl.semaphore_signal(
                    barrier, inc=1, device_id=(clu, other), device_id_type=MESH
                )

            return 0

        lax.fori_loop(1, members, greet, 0)

    @pl.when(jnp.logical_not(hub_chip))
    def _():
        for which in (0, 1):
            pl.semaphore_signal(
                barrier, inc=1, device_id=(clu, hub_mem(which) + 1), device_id_type=MESH
            )

    load_order.wait()
    load_emb.wait()

    def fetch(s):
        return emb_ref[order_ref[0, mem * PER + s]]

    def share(which, c):
        seen = mirrored(which, chip)
        _, slot = base_and_slot(which, seen, c)
        return pltpu.make_async_remote_copy(
            src_ref=mine.at[which * HALF + c],
            dst_ref=buf.at[slot, pl.ds(pl.multiple_of(core * BLK, BLK), BLK)],
            send_sem=send_sem.at[which, c],
            recv_sem=recv_sem.at[slot, core],
            device_id=(clu, hub_mem(which) + jnp.where(seen < mid - 1, 0, 1)),
            device_id_type=MESH,
        )

    def at_event(e):
        i = e - HALF
        j = i - HALF * mid
        idx = i % mid
        near = jnp.where(idx == 0, mid - 1, mid + idx)
        seen = jnp.where(i < 0, mid, jnp.where(j < 0, near, j % (mid - 1)))
        c = jnp.where(i < 0, e, jnp.where(j < 0, i // mid, j // (mid - 1)))
        return base_and_slot(role, seen, c)

    def arrived(slot, half):
        pltpu.make_async_remote_copy(
            src_ref=mine.at[0],
            dst_ref=buf.at[slot, pl.ds(half * BLK, BLK)],
            send_sem=send_sem.at[0, 0],
            recv_sem=recv_sem.at[slot, half],
            device_id=(clu, hub_mem(0)),
            device_id_type=MESH,
        ).wait_recv()

    def passed(slot):
        return pltpu.make_async_remote_copy(
            src_ref=buf.at[slot],
            dst_ref=buf.at[slot],
            send_sem=pass_send.at[slot],
            recv_sem=pass_recv.at[slot],
            device_id=(clu, 2 * chip),
            device_id_type=MESH,
        )

    part_copy = pltpu.make_async_remote_copy(
        src_ref=partial,
        dst_ref=partial,
        send_sem=part_sem.at[0],
        recv_sem=part_sem.at[1],
        device_id=(clu, 2 * chip),
        device_id_type=MESH,
    )

    def norms(slot):
        wide = buf[slot].astype(jnp.float32)
        turned[slot] = wide.T.astype(jnp.bfloat16)
        square = wide * wide
        part = square[:, :BLK]
        for k in range(1, square.shape[1] // BLK):
            part = part + square[:, k * BLK : (k + 1) * BLK]
        hrow[slot] = 0.5 * jnp.sum(part.T, axis=0, keepdims=True)
        colacc[slot] = jnp.zeros((2, 8, BLK), jnp.float32)
        return 0.5 * jnp.sum(part, axis=1, keepdims=True)

    def compare(base, slot, hcol):
        rowacc[...] = jnp.zeros_like(rowacc)
        left = jnp.broadcast_to(hcol, (UNIT, BLK))

        def tiles(q, count):
            for k in range(count):
                prod = lax.dot_general(
                    buf[slot], turned[q + k], (((1,), (0,)), ((), ())),
                    preferred_element_type=jnp.float32,
                )
                h = hrow[q + k]
                t0 = jnp.exp(prod[:, :BLK] - left - h[:, :BLK])
                t1 = jnp.exp(prod[:, BLK:] - left - h[:, BLK:])
                rowacc[...] += t0 + t1
                colacc[q + k, 0] += jnp.sum(t0.reshape(UNIT // 8, 8, BLK), axis=0)
                colacc[q + k, 1] += jnp.sum(t1.reshape(UNIT // 8, 8, BLK), axis=0)

        count = slot + 1 - base
        quads = count // 4

        def four(k, _):
            tiles(base + 4 * k, 4)
            return 0

        lax.fori_loop(0, quads, four, 0)

        @pl.when(count % 4 >= 2)
        def _():
            tiles(base + 4 * quads, 2)

        @pl.when(count % 2 == 1)
        def _():
            tiles(slot, 1)

        colacc[slot] = jnp.zeros((2, 8, BLK), jnp.float32)
        across[slot] = jnp.sum(rowacc[...].T, axis=0, keepdims=True)

    def density(slot):
        down = jnp.sum(colacc[slot], axis=1)
        return across[slot] + jnp.concatenate([down[:1], down[1:]], axis=1)

    @pl.when(jnp.logical_not(hub_chip))
    def _():
        pl.semaphore_wait(barrier, hubs + 2)
        first = jnp.where(chip < mid, 1, 0)

        def step(k, _):
            @pl.when(k < PER)
            def _():
                turn = k // HALF
                which = first * (1 - turn) + (1 - first) * turn
                mine[which * HALF + k % HALF] = fetch(which * HALF + k % HALF)
                share(which, k % HALF).start()

            @pl.when(k >= HALF)
            def _():
                done = k - HALF
                turn = done // HALF
                share(first * (1 - turn) + (1 - first) * turn, done % HALF).wait_send()

            return 0

        lax.fori_loop(0, PER + HALF, step, 0)

    @pl.when(is_near)
    def _():
        pl.semaphore_wait(barrier, hubs + members - 3)
        for c in range(HALF):
            mine[(1 - role) * HALF + c] = fetch((1 - role) * HALF + c)
            share(1 - role, c).start()
        for c in range(HALF):
            _, slot = base_and_slot(role, mid, c)
            buf[slot, BLK:] = fetch(role * HALF + c)
        partial[...] = jnp.zeros_like(partial)

        def receive(slot, e):
            arrived(slot, 0)

            @pl.when(e >= HALF)
            def _():
                arrived(slot, 1)

            passed(slot).start()

        def event(e, _):
            base, slot = at_event(e)
            receive(slot, e)
            compare(base, slot, norms(slot))
            return 0

        def forward(e, _):
            receive(at_event(e)[1], e)
            return 0

        def late_event(e, _):
            base, slot = at_event(e)
            compare(base, slot, norms(slot))
            return 0

        lax.fori_loop(0, near_events - HALF, event, 0)
        lax.fori_loop(near_events - HALF, near_events, forward, 0)
        lax.fori_loop(near_events - HALF, near_events, late_event, 0)

        def fill(e, _):
            _, slot = at_event(e)
            partial[pl.ds(slot, 1)] = density(slot)
            return 0

        lax.fori_loop(0, near_events, fill, 0)
        part_copy.start()

        def drain(e, _):
            _, slot = at_event(e)
            passed(slot).wait_send()
            return 0

        lax.fori_loop(0, near_events, drain, 0)
        for c in range(HALF):
            share(1 - role, c).wait_send()
        part_copy.wait_send()

    @pl.when(is_hub)
    def _():
        pl.semaphore_wait(barrier, everyone - 1)
        for which in (1 - role, role):
            for c in range(HALF):
                mine[which * HALF + c] = fetch(which * HALF + c)
                share(which, c).start()
        result[...] = jnp.zeros_like(result)

        def take(e, _):
            _, slot = at_event(e)
            passed(slot).wait_recv()
            norms(slot)
            across[slot] = jnp.zeros((1, UNIT), jnp.float32)
            return 0

        lax.fori_loop(0, near_events, take, 0)

        def event(e, _):
            base, slot = at_event(e)
            arrived(slot, 0)
            arrived(slot, 1)
            compare(base, slot, norms(slot))
            return 0

        lax.fori_loop(near_events, events, event, 0)
        part_copy.wait_recv()

        def finish(seen, _):
            holder = mirrored(role, seen)
            for c in range(HALF):
                _, slot = base_and_slot(role, seen, c)
                inverse = 1.0 / (density(slot) + partial[pl.ds(slot, 1)])
                for half in (0, 1):
                    result[2 * holder + half, c : c + 1] = inverse[
                        :, half * BLK : (half + 1) * BLK
                    ]
            return 0

        lax.fori_loop(0, chips, finish, 0)
        own = jnp.sum(jnp.sum(result[...], axis=0), axis=0, keepdims=True)
        result[:, HALF : HALF + 1] = jnp.broadcast_to(own[None], (members, 1, BLK))

        def back(k):
            other = (mem + k) % members
            return pltpu.make_async_remote_copy(
                src_ref=result.at[other],
                dst_ref=weights.at[role],
                send_sem=back_send.at[k],
                recv_sem=back_recv.at[role],
                device_id=(clu, other),
                device_id_type=MESH,
            )

        def sum_copy(k):
            flat = (clu * members + k) % everyone
            return pltpu.make_async_remote_copy(
                src_ref=result.at[mem],
                dst_ref=sums.at[2 * clu + role],
                send_sem=sum_send.at[k],
                recv_sem=sum_recv.at[2 * clu + role],
                device_id=(flat // members, flat % members),
                device_id_type=MESH,
            )

        def tell(k, _):
            sum_copy(k).start()
            return 0

        def told(k, _):
            sum_copy(k).wait_send()
            return 0

        lax.fori_loop(members, everyone, tell, 0)
        for k in range(1, members):
            back(k).start()
        weights[role] = result[mem]
        for c in range(HALF):
            share(role, c).wait_send()
            share(1 - role, c).wait_send()
        lax.fori_loop(members, everyone, told, 0)
        for k in range(1, members):
            back(k).wait_send()

    def returned(which):
        pltpu.make_async_remote_copy(
            src_ref=result.at[0],
            dst_ref=weights.at[which],
            send_sem=back_send.at[0],
            recv_sem=back_recv.at[which],
            device_id=(clu, hub_mem(which)),
            device_id_type=MESH,
        ).wait_recv()

    for which in (0, 1):
        @pl.when(mem != hub_mem(which))
        def _(which=which):
            returned(which)

    for one in range(hubs):
        @pl.when(clu == one // 2)
        def _(one=one):
            sums[one] = weights[one % 2]

        @pl.when(clu != one // 2)
        def _(one=one):
            pltpu.make_async_remote_copy(
                src_ref=sums.at[one],
                dst_ref=sums.at[one],
                send_sem=sum_send.at[0],
                recv_sem=sum_recv.at[one],
                device_id=(clu, hub_mem(0)),
                device_id_type=MESH,
            ).wait_recv()

    total = jnp.sum(jnp.sum(sums[...], axis=0)[HALF : HALF + 1], keepdims=True)
    scale = float(everyone * PER * BLK) / total
    for block in range(PER):
        spot = 0
        for s in range(PER):
            spot = jnp.where(order_ref[0, mem * PER + s] == block, s, spot)
        out_ref[block : block + 1] = weights[spot // HALF, pl.ds(spot % HALF, 1)] * scale


def solution(mesh):
    groups, members = mesh.shape["clu"], mesh.shape["mem"]

    def shards(embeddings, block_order):
        rows, width = embeddings.shape
        units = HALF * members // 2
        out = pl.pallas_call(
            functools.partial(kernel, groups, members),
            out_shape=jax.ShapeDtypeStruct((PER, BLK), jnp.float32),
            in_specs=[pl.BlockSpec(memory_space=pl.ANY)] * 2,
            out_specs=pl.BlockSpec(memory_space=pltpu.VMEM),
            scratch_shapes=[
                pltpu.SMEM(block_order.shape, jnp.int32),
                pltpu.VMEM((PER, BLK, width), jnp.bfloat16),
                pltpu.SemaphoreType.DMA((2,)),
                pltpu.VMEM((PER, BLK, width), jnp.bfloat16),
                pltpu.VMEM((units, UNIT, width), jnp.bfloat16),
                pltpu.VMEM((units, width, UNIT), jnp.bfloat16),
                pltpu.VMEM((UNIT, BLK), jnp.float32),
                pltpu.VMEM((units, 2, 8, BLK), jnp.float32),
                pltpu.VMEM((units, 1, UNIT), jnp.float32),
                pltpu.VMEM((units, 1, UNIT), jnp.float32),
                pltpu.VMEM((members, 8, BLK), jnp.float32),
                pltpu.VMEM((2 * groups, 8, BLK), jnp.float32),
                pltpu.VMEM((2, 8, BLK), jnp.float32),
                pltpu.VMEM((units, UNIT), jnp.float32),
                pltpu.SemaphoreType.DMA((2, HALF)),
                pltpu.SemaphoreType.DMA((units, 2)),
                pltpu.SemaphoreType.DMA((units,)),
                pltpu.SemaphoreType.DMA((units,)),
                pltpu.SemaphoreType.DMA((2,)),
                pltpu.SemaphoreType.DMA((groups * members,)),
                pltpu.SemaphoreType.DMA((2 * groups,)),
                pltpu.SemaphoreType.DMA((members,)),
                pltpu.SemaphoreType.DMA((2,)),
            ],
            compiler_params=pltpu.CompilerParams(
                collective_id=0, has_side_effects=True, vmem_limit_bytes=58 * 1024 * 1024
            ),
            cost_estimate=pl.CostEstimate(
                flops=2 * rows * rows * members * width // 6,
                bytes_accessed=rows * width * 2,
                transcendentals=rows * rows,
            ),
        )(block_order, embeddings.reshape(PER, BLK, width))
        return out.reshape(rows)

    return jax.shard_map(
        shards,
        mesh=mesh,
        in_specs=(P(("clu", "mem"), None), P("clu", None)),
        out_specs=P(("clu", "mem")),
        check_vma=False,
    )
```

```python
import functools

import jax
import jax.numpy as jnp
from jax import lax
from jax.experimental import pallas as pl
from jax.experimental.pallas import tpu as pltpu
from jax.sharding import PartitionSpec as P

BLK = 128
PER = 8
HALF = PER // 2
UNIT = 2 * BLK
MESH = pl.DeviceIdType.MESH


def kernel(
    groups, members, order_hbm, emb_hbm, out_ref,
    order_ref, emb_ref, load_sem, mine, buf, turned, rowacc, colacc, across, hrow, result, sums, weights,
    partial, send_sem, recv_sem, pass_send, pass_recv, part_sem, sum_send, sum_recv, back_send, back_recv,
):
    chips = members // 2
    mid = chips // 2
    clu = lax.axis_index("clu")
    mem = lax.axis_index("mem")
    chip, core = mem // 2, mem % 2

    def hub_mem(which):
        return 2 * (mid - which)

    def mirrored(which, one_chip):
        return which * (chips - 1) + (1 - 2 * which) * one_chip

    def base_and_slot(which, seen, c):
        first = which * (c // 2) * c
        per_chip = HALF * (1 - which) + which * (2 - c // 2)
        cc = c - first
        near = per_chip + cc * mid + jnp.where(seen < mid, 0, seen - mid)
        far = per_chip + per_chip * mid + cc * (mid - 1) + seen
        place = jnp.where(seen == mid, cc, jnp.where(seen < mid - 1, far, near))
        return first * chips, first * chips + place

    hub_chip = jnp.logical_or(chip == mid, chip == mid - 1)
    is_hub = jnp.logical_and(hub_chip, core == 0)
    is_near = jnp.logical_and(hub_chip, core == 1)
    role = jnp.where(chip == mid - 1, 1, 0)
    hubs = 2 * groups
    everyone = groups * members
    events = HALF * chips
    near_events = HALF + HALF * mid

    load_order = pltpu.make_async_copy(order_hbm, order_ref, load_sem.at[0])
    load_emb = pltpu.make_async_copy(emb_hbm, emb_ref, load_sem.at[1])
    load_order.start()
    load_emb.start()
    barrier = pltpu.get_barrier_semaphore()

    @pl.when(is_hub)
    def _():
        def greet_all(k, _):
            flat = (clu * members + mem + k) % everyone
            pl.semaphore_signal(
                barrier, inc=1, device_id=(flat // members, flat % members),
                device_id_type=MESH,
            )
            return 0

        lax.fori_loop(1, everyone, greet_all, 0)

    @pl.when(jnp.logical_not(is_hub))
    def _():
        def greet_hub(g, _):
            for which in (0, 1):
                pl.semaphore_signal(
                    barrier, inc=1, device_id=(g, hub_mem(which)), device_id_type=MESH
                )
            return 0

        lax.fori_loop(0, groups, greet_hub, 0)

    @pl.when(is_near)
    def _():
        def greet(k, _):
            other = (mem + k) % members

            @pl.when(jnp.logical_and(other != hub_mem(0), other != hub_mem(1)))
            def _():
                pl.semaphore_signal(
                    barrier, inc=1, device_id=(clu, other), device_id_type=MESH
                )

            return 0

        lax.fori_loop(1, members, greet, 0)

    @pl.when(jnp.logical_not(hub_chip))
    def _():
        for which in (0, 1):
            pl.semaphore_signal(
                barrier, inc=1, device_id=(clu, hub_mem(which) + 1), device_id_type=MESH
            )

    load_order.wait()
    load_emb.wait()
    for s in range(PER):
        mine[s] = emb_ref[order_ref[0, mem * PER + s]]

    def share(which, c):
        seen = mirrored(which, chip)
        _, slot = base_and_slot(which, seen, c)
        return pltpu.make_async_remote_copy(
            src_ref=mine.at[which * HALF + c],
            dst_ref=buf.at[slot, pl.ds(pl.multiple_of(core * BLK, BLK), BLK)],
            send_sem=send_sem.at[which, c],
            recv_sem=recv_sem.at[slot, core],
            device_id=(clu, hub_mem(which) + jnp.where(seen < mid - 1, 0, 1)),
            device_id_type=MESH,
        )

    def at_event(e):
        i = e - HALF
        j = i - HALF * mid
        idx = i % mid
        near = jnp.where(idx == 0, mid - 1, mid + idx)
        seen = jnp.where(i < 0, mid, jnp.where(j < 0, near, j % (mid - 1)))
        c = jnp.where(i < 0, e, jnp.where(j < 0, i // mid, j // (mid - 1)))
        return base_and_slot(role, seen, c)

    def arrived(slot, half):
        pltpu.make_async_remote_copy(
            src_ref=mine.at[0],
            dst_ref=buf.at[slot, pl.ds(half * BLK, BLK)],
            send_sem=send_sem.at[0, 0],
            recv_sem=recv_sem.at[slot, half],
            device_id=(clu, hub_mem(0)),
            device_id_type=MESH,
        ).wait_recv()

    def passed(slot):
        return pltpu.make_async_remote_copy(
            src_ref=buf.at[slot],
            dst_ref=buf.at[slot],
            send_sem=pass_send.at[slot],
            recv_sem=pass_recv.at[slot],
            device_id=(clu, 2 * chip),
            device_id_type=MESH,
        )

    part_copy = pltpu.make_async_remote_copy(
        src_ref=partial,
        dst_ref=partial,
        send_sem=part_sem.at[0],
        recv_sem=part_sem.at[1],
        device_id=(clu, 2 * chip),
        device_id_type=MESH,
    )

    def norms(slot):
        wide = buf[slot].astype(jnp.float32)
        turned[slot] = wide.T.astype(jnp.bfloat16)
        square = wide * wide
        part = square[:, :BLK]
        for k in range(1, square.shape[1] // BLK):
            part = part + square[:, k * BLK : (k + 1) * BLK]
        hrow[slot] = 0.5 * jnp.sum(part.T, axis=0, keepdims=True)
        colacc[slot] = jnp.zeros((2, 8, BLK), jnp.float32)
        return 0.5 * jnp.sum(part, axis=1, keepdims=True)

    def compare(base, slot, hcol):
        rowacc[...] = jnp.zeros_like(rowacc)
        left = jnp.broadcast_to(hcol, (UNIT, BLK))

        def tiles(q, count):
            for k in range(count):
                prod = lax.dot_general(
                    buf[slot], turned[q + k], (((1,), (0,)), ((), ())),
                    preferred_element_type=jnp.float32,
                )
                h = hrow[q + k]
                t0 = jnp.exp(prod[:, :BLK] - left - h[:, :BLK])
                t1 = jnp.exp(prod[:, BLK:] - left - h[:, BLK:])
                rowacc[...] += t0 + t1
                colacc[q + k, 0] += jnp.sum(t0.reshape(UNIT // 8, 8, BLK), axis=0)
                colacc[q + k, 1] += jnp.sum(t1.reshape(UNIT // 8, 8, BLK), axis=0)

        count = slot + 1 - base
        quads = count // 4

        def four(k, _):
            tiles(base + 4 * k, 4)
            return 0

        lax.fori_loop(0, quads, four, 0)

        @pl.when(count % 4 >= 2)
        def _():
            tiles(base + 4 * quads, 2)

        @pl.when(count % 2 == 1)
        def _():
            tiles(slot, 1)

        colacc[slot] = jnp.zeros((2, 8, BLK), jnp.float32)
        across[slot] = jnp.sum(rowacc[...].T, axis=0, keepdims=True)

    def density(slot):
        down = jnp.sum(colacc[slot], axis=1)
        return across[slot] + jnp.concatenate([down[:1], down[1:]], axis=1)

    @pl.when(jnp.logical_not(hub_chip))
    def _():
        pl.semaphore_wait(barrier, hubs + 2)
        first = jnp.where(chip < mid, 1, 0)

        def step(k, _):
            @pl.when(k < PER)
            def _():
                turn = k // HALF
                share(first * (1 - turn) + (1 - first) * turn, k % HALF).start()

            @pl.when(k >= HALF)
            def _():
                done = k - HALF
                turn = done // HALF
                share(first * (1 - turn) + (1 - first) * turn, done % HALF).wait_send()

            return 0

        lax.fori_loop(0, PER + HALF, step, 0)

    @pl.when(is_near)
    def _():
        pl.semaphore_wait(barrier, hubs + members - 3)
        for c in range(HALF):
            share(1 - role, c).start()
        for c in range(HALF):
            _, slot = base_and_slot(role, mid, c)
            buf[slot, BLK:] = mine[role * HALF + c]
        partial[...] = jnp.zeros_like(partial)

        def event(e, _):
            base, slot = at_event(e)
            arrived(slot, 0)

            @pl.when(e >= HALF)
            def _():
                arrived(slot, 1)

            passed(slot).start()
            compare(base, slot, norms(slot))
            return 0

        lax.fori_loop(0, near_events, event, 0)

        def fill(e, _):
            _, slot = at_event(e)
            partial[pl.ds(slot, 1)] = density(slot)
            return 0

        lax.fori_loop(0, near_events, fill, 0)
        part_copy.start()

        def drain(e, _):
            _, slot = at_event(e)
            passed(slot).wait_send()
            return 0

        lax.fori_loop(0, near_events, drain, 0)
        for c in range(HALF):
            share(1 - role, c).wait_send()
        part_copy.wait_send()

    @pl.when(is_hub)
    def _():
        pl.semaphore_wait(barrier, everyone - 1)
        for c in range(HALF):
            share(role, c).start()
        for c in range(HALF):
            share(1 - role, c).start()
        result[...] = jnp.zeros_like(result)

        def take(e, _):
            _, slot = at_event(e)
            passed(slot).wait_recv()
            norms(slot)
            across[slot] = jnp.zeros((1, UNIT), jnp.float32)
            return 0

        lax.fori_loop(0, near_events, take, 0)

        def event(e, _):
            base, slot = at_event(e)
            arrived(slot, 0)
            arrived(slot, 1)
            compare(base, slot, norms(slot))
            return 0

        lax.fori_loop(near_events, events, event, 0)
        part_copy.wait_recv()

        def finish(seen, _):
            holder = mirrored(role, seen)
            for c in range(HALF):
                _, slot = base_and_slot(role, seen, c)
                inverse = 1.0 / (density(slot) + partial[pl.ds(slot, 1)])
                for half in (0, 1):
                    result[2 * holder + half, c : c + 1] = inverse[
                        :, half * BLK : (half + 1) * BLK
                    ]
            return 0

        lax.fori_loop(0, chips, finish, 0)
        sums[2 * clu + role] = jnp.sum(result[...], axis=0)

        def back(k):
            other = (mem + k) % members
            return pltpu.make_async_remote_copy(
                src_ref=result.at[other],
                dst_ref=weights.at[role],
                send_sem=back_send.at[k],
                recv_sem=back_recv.at[role],
                device_id=(clu, other),
                device_id_type=MESH,
            )

        def sum_copy(k):
            flat = (clu * members + mem + k) % everyone
            return pltpu.make_async_remote_copy(
                src_ref=sums.at[2 * clu + role],
                dst_ref=sums.at[2 * clu + role],
                send_sem=sum_send.at[k],
                recv_sem=sum_recv.at[2 * clu + role],
                device_id=(flat // members, flat % members),
                device_id_type=MESH,
            )

        def tell(k, _):
            sum_copy(k).start()
            return 0

        def told(k, _):
            sum_copy(k).wait_send()
            return 0

        lax.fori_loop(1, everyone, tell, 0)
        for k in range(1, members):
            back(k).start()
        weights[role] = result[mem]
        for c in range(HALF):
            share(role, c).wait_send()
            share(1 - role, c).wait_send()
        lax.fori_loop(1, everyone, told, 0)
        for k in range(1, members):
            back(k).wait_send()

    def returned(which):
        pltpu.make_async_remote_copy(
            src_ref=result.at[0],
            dst_ref=weights.at[which],
            send_sem=back_send.at[0],
            recv_sem=back_recv.at[which],
            device_id=(clu, hub_mem(which)),
            device_id_type=MESH,
        ).wait_recv()

    for which in (0, 1):
        @pl.when(mem != hub_mem(which))
        def _(which=which):
            returned(which)

    for one in range(hubs):
        @pl.when(jnp.logical_or(clu != one // 2, mem != hub_mem(one % 2)))
        def _(one=one):
            pltpu.make_async_remote_copy(
                src_ref=sums.at[one],
                dst_ref=sums.at[one],
                send_sem=sum_send.at[0],
                recv_sem=sum_recv.at[one],
                device_id=(clu, hub_mem(0)),
                device_id_type=MESH,
            ).wait_recv()

    total = jnp.sum(jnp.sum(sums[...], axis=0), keepdims=True)
    scale = float(everyone * PER * BLK) / total
    for block in range(PER):
        spot = 0
        for s in range(PER):
            spot = jnp.where(order_ref[0, mem * PER + s] == block, s, spot)
        out_ref[block : block + 1] = weights[spot // HALF, pl.ds(spot % HALF, 1)] * scale


def solution(mesh):
    groups, members = mesh.shape["clu"], mesh.shape["mem"]

    def shards(embeddings, block_order):
        rows, width = embeddings.shape
        units = HALF * members // 2
        out = pl.pallas_call(
            functools.partial(kernel, groups, members),
            out_shape=jax.ShapeDtypeStruct((PER, BLK), jnp.float32),
            in_specs=[pl.BlockSpec(memory_space=pl.ANY)] * 2,
            out_specs=pl.BlockSpec(memory_space=pltpu.VMEM),
            scratch_shapes=[
                pltpu.SMEM(block_order.shape, jnp.int32),
                pltpu.VMEM((PER, BLK, width), jnp.bfloat16),
                pltpu.SemaphoreType.DMA((2,)),
                pltpu.VMEM((PER, BLK, width), jnp.bfloat16),
                pltpu.VMEM((units, UNIT, width), jnp.bfloat16),
                pltpu.VMEM((units, width, UNIT), jnp.bfloat16),
                pltpu.VMEM((UNIT, BLK), jnp.float32),
                pltpu.VMEM((units, 2, 8, BLK), jnp.float32),
                pltpu.VMEM((units, 1, UNIT), jnp.float32),
                pltpu.VMEM((units, 1, UNIT), jnp.float32),
                pltpu.VMEM((members, 8, BLK), jnp.float32),
                pltpu.VMEM((2 * groups, 8, BLK), jnp.float32),
                pltpu.VMEM((2, 8, BLK), jnp.float32),
                pltpu.VMEM((units, UNIT), jnp.float32),
                pltpu.SemaphoreType.DMA((2, HALF)),
                pltpu.SemaphoreType.DMA((units, 2)),
                pltpu.SemaphoreType.DMA((units,)),
                pltpu.SemaphoreType.DMA((units,)),
                pltpu.SemaphoreType.DMA((2,)),
                pltpu.SemaphoreType.DMA((groups * members,)),
                pltpu.SemaphoreType.DMA((2 * groups,)),
                pltpu.SemaphoreType.DMA((members,)),
                pltpu.SemaphoreType.DMA((2,)),
            ],
            compiler_params=pltpu.CompilerParams(
                collective_id=0, has_side_effects=True, vmem_limit_bytes=53 * 1024 * 1024
            ),
            cost_estimate=pl.CostEstimate(
                flops=2 * rows * rows * members * width // 6,
                bytes_accessed=rows * width * 2,
                transcendentals=rows * rows,
            ),
        )(block_order, embeddings.reshape(PER, BLK, width))
        return out.reshape(rows)

    return jax.shard_map(
        shards,
        mesh=mesh,
        in_specs=(P(("clu", "mem"), None), P("clu", None)),
        out_specs=P(("clu", "mem")),
        check_vma=False,
    )
```
